32 devices in a mesh: grp: 4 (over z), dev: 8 (over y, x, core).
Axes of the slice: x: 2, y: 2, z: 4, core: 2. Of those that a mesh axis runs over, the one named last changes fastest.
Arguments:
- subspace: bfloat16 [64, 65536], P(None, ('grp', 'dev')), may hold values from -6 to 6
- tiles: bfloat16 [512, 16, 128, 128], P(('grp', 'dev')), as said below
- tile_count: int32 [512], P(('grp', 'dev')), may hold values from 1 to 16, as said below
- tile_slot: int32 [512, 16], P(('grp', 'dev')), may hold values from 0 to 15, as said below
- fetch_list: int32 [32, 8, 2], P(('grp', 'dev')), may hold values from 0 to 15, as said below
Outputs:
- orthonormal: float32 [64, 65536], P(None, ('grp', 'dev'))
The draws below stay inside these ranges and needn't reach their ends.
Inputs may be any that keep to these rules, and one draw needn't show every extreme that they name: `tile_count`: at least 1 and at most 16; every device has a block row with 16. `tile_slot`: each entry of a device's fetch list is named by some slot of that device. `fetch_list`: the 2 entries for one pair of devices differ. `tiles`: entries positive.
All inputs are finite; a program needn't handle non-finite values.
Results may differ from the reference program's by a relative error of at most 0.007.
Values may be sent and summed in bfloat16 or wider, within the bound.
No kernel may reach another device: no remote copies, remote signals or barrier semaphores. Data moves between devices by JAX's collectives and lax.ppermute only.
A program may use at most 64 MiB of HBM per device.

```python
import jax
import jax.numpy as jnp
from jax import lax

K = 64
TILE = 128
RB_DEV = 16
TPB = 16
CAP = 2
ROWBLOCKS = 512
ROWS = 65536
N_GRP = 4
N_DEV = 8
DEVICES = 32


def draw_tiles(key, part):
    key = jax.random.fold_in(key, 11)
    first_key = jax.random.fold_in(key, 0)
    shape = (ROWBLOCKS, TPB, TILE, TILE)
    values = jax.random.uniform(first_key, shape, jnp.float32, 0.05, 1.0)
    owner = jnp.arange(ROWBLOCKS) // RB_DEV
    dev_pos = (owner % N_DEV).astype(jnp.float32) / max(N_DEV - 1, 1)
    grp_pos = (owner // N_DEV).astype(jnp.float32) / max(N_GRP - 1, 1)
    scale = jnp.exp((dev_pos + grp_pos) * 2.1972)
    return (values * scale[:, None, None, None]).astype(jnp.bfloat16)


def draw_tile_count(key, part):
    key = jax.random.fold_in(key, 23)
    first_key, second_key, third_key = jax.random.split(key, 3)
    left = jax.random.randint(first_key, (ROWBLOCKS,), 0, TPB)
    right = jax.random.randint(second_key, (ROWBLOCKS,), 0, TPB)
    counts = jnp.minimum(1 + left * right // max(TPB // 2, 1), TPB)
    chosen = jax.random.randint(third_key, (DEVICES,), 0, RB_DEV)
    position = jnp.arange(ROWBLOCKS) % RB_DEV
    full_here = position == jnp.repeat(chosen, RB_DEV)
    return jnp.where(full_here, TPB, counts).astype(jnp.int32)


def draw_tile_slot(key, part):
    key = jax.random.fold_in(key, 37)
    width = RB_DEV * TPB
    scores = jax.random.randint(key, (DEVICES, width), 0, 2 ** 20) * width + jnp.arange(width)[None, :]
    order = jnp.argsort(scores, axis=1)
    return (order % (N_DEV * CAP)).reshape(ROWBLOCKS, TPB).astype(jnp.int32)


def draw_fetch_list(key, part):
    key = jax.random.fold_in(key, 53)
    scores = jax.random.randint(key, (DEVICES * N_DEV, RB_DEV), 0, 2 ** 20) * RB_DEV + jnp.arange(RB_DEV)[None, :]
    order = jnp.argsort(scores, axis=1)[:, :CAP]
    return order.reshape(DEVICES, N_DEV, CAP).astype(jnp.int32)


def shard_levels(stream_key, shape, cuts, smallest, largest):
    factor_of, own = 1.0, jax.random.fold_in(stream_key, 6)
    for dim, shards_of in cuts:
        heights = jnp.exp(jax.random.uniform(jax.random.fold_in(own, dim), (shards_of,), jnp.float32, smallest / len(cuts), largest / len(cuts)))
        factor_of = factor_of * jnp.repeat(heights, shape[dim] // shards_of).reshape([-1 if axis == dim else 1 for axis in range(len(shape))])
    return factor_of


def centred(own_key, extent, deviation, bound, cuts=(), kind=jnp.bfloat16):
    result = deviation * jax.random.normal(own_key, extent, jnp.float32)
    if cuts:
        result = result * shard_levels(own_key, extent, cuts, -0.22, 0.18)
    return jnp.clip(result, -bound, bound).astype(kind)


def setup_inputs(seed: int = 0) -> dict:
    keys = jax.random.split(jax.random.key(seed), 6)
    subspace = centred(keys[0], (K, ROWS), 1.0, 6.0, ((1, 32),))
    tiles = draw_tiles(jax.random.fold_in(keys[5], 71), 0)
    tile_count = draw_tile_count(jax.random.fold_in(keys[5], 71), 0)
    tile_slot = draw_tile_slot(jax.random.fold_in(keys[5], 71), 0)
    fetch_list = draw_fetch_list(jax.random.fold_in(keys[5], 71), 0)
    return {"subspace": subspace, "tiles": tiles, "tile_count": tile_count, "tile_slot": tile_slot, "fetch_list": fetch_list}


def reference(subspace, tiles, tile_count, tile_slot, fetch_list):
    live_mask = (jnp.arange(TPB, dtype=jnp.int32)[None, :] < tile_count[:, None]).astype(jnp.bfloat16)
    tiles_dev = tiles.reshape(DEVICES, RB_DEV, TPB, TILE, TILE)
    live_dev = live_mask.reshape(DEVICES, RB_DEV, TPB)

    def degree_of(packed):
        tile_part, mask_part = packed
        return jnp.einsum('btrc,bt->br', tile_part.astype(jnp.float32), mask_part.astype(jnp.float32))
    degree = lax.map(degree_of, (tiles_dev, live_dev)).reshape(ROWS)
    inv_root = lax.rsqrt(degree)
    scaled = (subspace.astype(jnp.float32) * inv_root[None, :]).astype(jnp.bfloat16)
    blocks_all = scaled.reshape(K, ROWBLOCKS, TILE)
    device_ids = jnp.arange(DEVICES, dtype=jnp.int32)
    group_ids = device_ids // N_DEV
    flat_lists = fetch_list.reshape(DEVICES, N_DEV * CAP)
    slots_dev = tile_slot.reshape(DEVICES, RB_DEV * TPB)
    local_col = jnp.take_along_axis(flat_lists, slots_dev, axis=1)
    columns = ((group_ids[:, None] * N_DEV + slots_dev // CAP) * RB_DEV + local_col).astype(jnp.int32)

    def product_of(packed):
        tile_part, mask_part, col_part = packed
        operand = jnp.take(blocks_all, col_part, axis=1).reshape(K, RB_DEV, TPB, TILE)
        operand = operand * mask_part[None, :, :, None]
        return jnp.einsum('kbtc,btrc->kbr', operand.astype(jnp.float32), tile_part.astype(jnp.float32))
    products = lax.map(product_of, (tiles_dev, live_dev, columns))
    applied = jnp.transpose(products, (1, 0, 2, 3)).reshape(K, ROWS) * inv_root[None, :]
    gram = jnp.dot(applied, applied.T, precision=lax.Precision.HIGHEST)
    factor = jnp.linalg.cholesky(gram)
    return jax.scipy.linalg.solve_triangular(factor, applied, lower=True)
```

```python
import functools

import jax
import jax.numpy as jnp
from jax import lax
from jax.experimental import pallas as pl
from jax.experimental.pallas import tpu as pltpu
from jax.sharding import PartitionSpec as P

CHUNK = 4
VMEM = pl.BlockSpec(memory_space=pltpu.VMEM)
SMEM = pl.BlockSpec(memory_space=pltpu.SMEM)
NT = (((1,), (1,)), ((), ()))


def degree_kernel(count_ref, tiles_ref, sub_ref, scaled_ref, inv_ref, held_ref, sems):
    blocks, slots, rows, cols = tiles_ref.shape
    chunks = slots // CHUNK

    def copy(b, c):
        part = pl.ds(c * CHUNK, CHUNK)
        return pltpu.make_async_copy(
            tiles_ref.at[b, part], held_ref.at[b, part], sems.at[b, c]
        )

    for b in range(blocks):
        for c in range(chunks):

            @pl.when(c * CHUNK < count_ref[b])
            def _():
                copy(b, c).start()

    ones = jnp.ones((8, cols), jnp.bfloat16)
    for b in range(blocks):
        count = count_ref[b]

        def add(c, total):
            copy(b, c).wait()
            for t in range(CHUNK):
                tile = held_ref[b, c * CHUNK + t].astype(jnp.float32)
                total = total + jnp.where(c * CHUNK + t < count, tile, 0.0)
            return total

        total = lax.fori_loop(
            0, pl.cdiv(count, CHUNK), add, jnp.zeros((rows, cols), jnp.float32)
        )
        high = total.astype(jnp.bfloat16)
        low = (total - high.astype(jnp.float32)).astype(jnp.bfloat16)
        degree = lax.dot_general(ones, high, NT, preferred_element_type=jnp.float32)
        degree = degree + lax.dot_general(ones, low, NT, preferred_element_type=jnp.float32)
        inv = lax.rsqrt(degree)
        lanes = slice(b * rows, (b + 1) * rows)
        inv_ref[:, lanes] = inv
        scaled_ref[b] = (sub_ref[:, lanes].astype(jnp.float32) * inv[:1]).astype(jnp.bfloat16)


def select_kernel(me_ref, lists_ref, scaled_ref, *send_refs):
    cap = send_refs[0].shape[1]
    me = me_ref[0]
    for i, send in enumerate(send_refs):
        for core in range(2):
            for j in range(cap):
                block = lists_ref[2 * i + core, me * cap + j]
                send[core, j] = scaled_ref[block]


def product_kernel(me_ref, count_ref, slot_ref, inv_ref, held_ref, own_ref, *refs):
    *near_refs, far_ref, applied_ref, gram_ref, table = refs
    blocks, slots, rows, cols = held_ref.shape
    cap, k_dim, _ = own_ref.shape[1:]
    me = me_ref[0]
    for i, near in enumerate([own_ref, *near_refs]):
        for j in range(cap):
            table[2 * i * cap + j] = near[0, j]
            table[(2 * i + 1) * cap + j] = far_ref[i, j]
    for b in range(blocks):
        count = count_ref[b]

        def add(c, total):
            parts, tiles = [], []
            for t in range(CHUNK):
                slot = slot_ref[b, c * CHUNK + t]
                entry = (lax.div(slot, cap) ^ me) * cap + lax.rem(slot, cap)
                operand = table[entry]
                parts.append(
                    jnp.where(c * CHUNK + t < count, operand, jnp.zeros_like(operand))
                )
                tiles.append(held_ref[b, c * CHUNK + t])
            return total + lax.dot_general(
                jnp.concatenate(parts, axis=1),
                jnp.concatenate(tiles, axis=1),
                NT,
                preferred_element_type=jnp.float32,
            )

        total = lax.fori_loop(
            0, pl.cdiv(count, CHUNK), add, jnp.zeros((k_dim, rows), jnp.float32)
        )
        lanes = slice(b * rows, (b + 1) * rows)
        applied_ref[:, lanes] = total * inv_ref[:1, lanes]
    applied = applied_ref[...]
    high = applied.astype(jnp.bfloat16)
    low = (applied - high.astype(jnp.float32)).astype(jnp.bfloat16)
    both = jnp.concatenate([high, low], axis=0)
    wide = lax.dot_general(both, both, NT, preferred_element_type=jnp.float32)
    wide = wide[:k_dim] + wide[k_dim:]
    gram = wide[:, :k_dim] + wide[:, k_dim:]
    half = k_dim // 2
    gram_ref[...] = jnp.concatenate([gram[:half], gram[half:]], axis=1)


def solve_kernel(here_ref, there_ref, applied_ref, out_ref):
    half, wide = here_ref.shape
    k_dim = wide // 2
    packed = here_ref[...] + there_ref[...]
    gram = jnp.concatenate([packed[:, :k_dim], packed[:, k_dim:]], axis=0)
    eye = (
        lax.broadcasted_iota(jnp.int32, (k_dim, k_dim), 0)
        == lax.broadcasted_iota(jnp.int32, (k_dim, k_dim), 1)
    ).astype(jnp.float32)
    whole = jnp.concatenate([gram, eye], axis=1)
    groups = [whole[8 * i : 8 * i + 8] for i in range(k_dim // 8)]
    row_ids = lax.broadcasted_iota(jnp.int32, (8, 1), 0)
    for j in range(k_dim):
        g, s = divmod(j, 8)
        row = groups[g][s : s + 1]
        step = row / row[:, j : j + 1]
        for i in range(g, k_dim // 8):
            column = groups[i][:, j : j + 1]
            if i == g:
                column = jnp.where(row_ids > s, column, 0.0)
            groups[i] = groups[i] - column * step
    whole = jnp.concatenate(groups, axis=0)
    diagonal = jnp.sum(whole[:, :k_dim] * eye, axis=1, keepdims=True)
    inverse = whole[:, k_dim:] * lax.rsqrt(diagonal)
    out_ref[...] = jnp.dot(
        inverse,
        applied_ref[...],
        precision=lax.Precision.HIGHEST,
        preferred_element_type=jnp.float32,
    )


def swap(x, axis, mask):
    size = lax.axis_size(axis)
    return lax.ppermute(x, axis, [(i, i ^ mask) for i in range(size)])


def bits(axis):
    size = lax.axis_size(axis)
    return [1 << i for i in range(size.bit_length() - 1)]


def body(subspace, tiles, tile_count, tile_slot, fetch_list):
    k_dim, row_count = subspace.shape
    blocks, slots, rows, cols = tiles.shape
    peers = lax.axis_size("dev")
    cap = fetch_list.shape[2]
    chips = peers // 2
    me = lax.axis_index("dev").astype(jnp.int32).reshape(1)

    lists = fetch_list.reshape(1, peers * cap)
    for mask in bits("dev"):
        lists = jnp.concatenate([lists, swap(lists, "dev", mask)], axis=0)

    scaled, inv_root, held = pl.pallas_call(
        degree_kernel,
        out_shape=(
            jax.ShapeDtypeStruct((blocks, k_dim, cols), jnp.bfloat16),
            jax.ShapeDtypeStruct((8, row_count), jnp.float32),
            pltpu.VMEM(tiles.shape, tiles.dtype),
        ),
        in_specs=[SMEM, pl.BlockSpec(memory_space=pl.ANY), VMEM],
        out_specs=(VMEM, VMEM, VMEM),
        scratch_shapes=[pltpu.SemaphoreType.DMA((blocks, slots // CHUNK))],
        compiler_params=pltpu.CompilerParams(vmem_limit_bytes=24 << 20),
        cost_estimate=pl.CostEstimate(
            flops=2 * tiles.size, bytes_accessed=2 * tiles.size, transcendentals=0
        ),
        name="degree",
    )(tile_count, tiles, subspace)

    sends = pl.pallas_call(
        select_kernel,
        out_shape=[jax.ShapeDtypeStruct((2, cap, k_dim, cols), jnp.bfloat16)] * chips,
        in_specs=[SMEM, SMEM, VMEM],
        out_specs=[VMEM] * chips,
        name="select",
    )(me, lists, scaled)

    own = sends[0]
    near = [swap(sends[i], "dev", 2 * i) for i in range(1, chips)]
    far = swap(jnp.stack([part[1] for part in [own, *near]]), "dev", 1)

    applied, gram = pl.pallas_call(
        product_kernel,
        out_shape=(
            jax.ShapeDtypeStruct((k_dim, row_count), jnp.float32),
            jax.ShapeDtypeStruct((k_dim // 2, 2 * k_dim), jnp.float32),
        ),
        in_specs=[SMEM, SMEM, SMEM] + [VMEM] * (chips + 3),
        out_specs=(VMEM, VMEM),
        scratch_shapes=[pltpu.VMEM((peers * cap, k_dim, cols), jnp.bfloat16)],
        compiler_params=pltpu.CompilerParams(vmem_limit_bytes=24 << 20),
        cost_estimate=pl.CostEstimate(
            flops=2 * tiles.size * k_dim, bytes_accessed=row_count * k_dim * 4, transcendentals=0
        ),
        name="product",
    )(me, tile_count, tile_slot, inv_root, held, own, *near, far)

    stages = [("dev", mask) for mask in bits("dev")] + [("grp", mask) for mask in bits("grp")]
    for axis, mask in stages[:-1]:
        gram = gram + swap(gram, axis, mask)
    other = swap(gram, *stages[-1])

    return pl.pallas_call(
        solve_kernel,
        out_shape=jax.ShapeDtypeStruct((k_dim, row_count), jnp.float32),
        in_specs=[VMEM] * 3,
        out_specs=VMEM,
        name="solve",
    )(gram, other, applied)


def solution(mesh):
    placed = (
        P(None, ("grp", "dev")),
        P(("grp", "dev"), None, None, None),
        P(("grp", "dev")),
        P(("grp", "dev"), None),
        P(("grp", "dev"), None, None),
    )
    return jax.shard_map(
        body, mesh=mesh, in_specs=placed, out_specs=P(None, ("grp", "dev")), check_vma=False
    )
```

```python
import jax
import jax.numpy as jnp
from jax import lax
from jax.experimental import pallas as pl
from jax.experimental.pallas import tpu as pltpu
from jax.sharding import PartitionSpec as P

VMEM = pl.BlockSpec(memory_space=pltpu.VMEM)
SMEM = pl.BlockSpec(memory_space=pltpu.SMEM)
NT = (((1,), (1,)), ((), ()))
F32 = jnp.float32
BF16 = jnp.bfloat16


def limit(mib):
    return pltpu.CompilerParams(vmem_limit_bytes=mib << 20)


def split(x):
    high = x.astype(BF16)
    return high, (x - high.astype(F32)).astype(BF16)


def degree_kernel(count_ref, tiles_ref, sub_ref, scaled_ref, inv_ref):
    blocks, slots, rows, cols = tiles_ref.shape
    slot_of_lane = lax.broadcasted_iota(jnp.int32, (8, slots * cols), 1) // cols
    for b in range(blocks):
        live = (slot_of_lane < count_ref[b]).astype(F32).astype(BF16)
        row = jnp.concatenate([tiles_ref[b, t] for t in range(slots)], axis=1)
        degree = lax.dot_general(live, row, NT, preferred_element_type=F32)
        inv = lax.rsqrt(degree)
        lanes = slice(b * rows, (b + 1) * rows)
        inv_ref[:, lanes] = inv
        scaled_ref[b] = (sub_ref[:, lanes].astype(F32) * inv[:1]).astype(BF16)


def select_kernel(me_ref, lists_ref, scaled_ref, *send_refs):
    cap = send_refs[0].shape[1]
    me = me_ref[0]
    for i, send in enumerate(send_refs):
        for core in range(2):
            for j in range(cap):
                block = lists_ref[2 * i + core, me * cap + j]
                send[core, j] = scaled_ref[block]


def product_kernel(me_ref, count_ref, slot_ref, inv_ref, tiles_ref, own_ref, *refs):
    *near_refs, far_ref, applied_ref, gram_ref, table = refs
    blocks, slots, rows, cols = tiles_ref.shape
    cap, k_dim, _ = own_ref.shape[1:]
    me = me_ref[0]
    for i, near in enumerate([own_ref, *near_refs]):
        for j in range(cap):
            table[2 * i * cap + j] = near[0, j]
            table[(2 * i + 1) * cap + j] = far_ref[i, j]
    for b in range(blocks):
        parts = []
        for t in range(slots):
            slot = slot_ref[b, t]
            entry = (lax.div(slot, cap) ^ me) * cap + lax.rem(slot, cap)
            block = table[entry]
            parts.append(jnp.where(t < count_ref[b], block, jnp.zeros_like(block)))
        row = jnp.concatenate([tiles_ref[b, t] for t in range(slots)], axis=1)
        total = lax.dot_general(
            jnp.concatenate(parts, axis=1), row, NT, preferred_element_type=F32
        )
        lanes = slice(b * rows, (b + 1) * rows)
        high, low = split(total * inv_ref[:1, lanes])
        applied_ref[:k_dim, lanes] = high
        applied_ref[k_dim:, lanes] = low
    both = applied_ref[...]
    wide = lax.dot_general(both, both, NT, preferred_element_type=F32)
    wide = wide[:k_dim] + wide[k_dim:]
    gram = wide[:, :k_dim] + wide[:, k_dim:]
    half = k_dim // 2
    gram_ref[...] = jnp.concatenate([gram[:half], gram[half:]], axis=1)


def inverse_factor(gram):
    k_dim = gram.shape[0]
    wide, groups = 2 * k_dim, k_dim // 8
    square = (k_dim, k_dim)
    eye = (
        lax.broadcasted_iota(jnp.int32, square, 0) == lax.broadcasted_iota(jnp.int32, square, 1)
    ).astype(F32)
    diagonal = gram * eye
    row_scale = lax.rsqrt(jnp.sum(diagonal, axis=1, keepdims=True))
    col_scale = lax.rsqrt(jnp.sum(diagonal, axis=0, keepdims=True))
    whole = jnp.concatenate([gram * row_scale * col_scale, eye * col_scale], axis=1)
    rows = [whole[8 * i : 8 * i + 8] for i in range(groups)]
    row_ids = lax.broadcasted_iota(jnp.int32, (8, wide), 0)

    def spread(x):
        return jnp.broadcast_to(x, (8, wide))

    done = []
    for g in range(groups):
        column = {
            (i, b): spread(rows[i][:, 8 * g + b : 8 * g + b + 1])
            for i in range(g, groups)
            for b in range(8)
        }
        out = rows[g]
        for s in range(0, 8, 2):
            row0, row1 = spread(rows[g][s : s + 1]), spread(rows[g][s + 1 : s + 2])
            pivot0 = {b: spread(column[g, b][s : s + 1]) for b in range(s, 8)}
            pivot1 = {b: spread(column[g, b][s + 1 : s + 2]) for b in range(s, 8)}
            p00, p01, p11 = pivot0[s], pivot0[s + 1], pivot1[s + 1]
            det = p00 * p11 - p01 * p01
            inv_det = pl.reciprocal(det, approx=True)
            inv_det = inv_det * (2.0 - det * inv_det)
            q00, q01, q11 = p11 * inv_det, p01 * inv_det, p00 * inv_det
            root0 = lax.rsqrt(p00)
            ratio = p01 * (root0 * root0)
            root1 = lax.rsqrt(p11 - p01 * ratio)
            out = jnp.where(row_ids == s, row0 * root0, out)
            out = jnp.where(row_ids == s + 1, (row1 - ratio * row0) * root1, out)
            for i in range(g, groups):
                x, y = column[i, s], column[i, s + 1]
                f0, f1 = q00 * x - q01 * y, q11 * y - q01 * x
                if i == g:
                    f0 = jnp.where(row_ids > s + 1, f0, 0.0)
                    f1 = jnp.where(row_ids > s + 1, f1, 0.0)
                rows[i] = rows[i] - f0 * row0 - f1 * row1
                for b in range(s + 2, 8):
                    column[i, b] = column[i, b] - f0 * pivot0[b] - f1 * pivot1[b]
        done.append(out)
    return jnp.concatenate(done, axis=0)[:, k_dim:]


def solve_kernel(here_ref, there_ref, applied_ref, out_ref):
    k_dim = here_ref.shape[1] // 2
    packed = here_ref[...] + there_ref[...]
    gram = jnp.concatenate([packed[:, :k_dim], packed[:, k_dim:]], axis=0)
    high, low = split(inverse_factor(gram))
    out_ref[...] = jnp.dot(
        jnp.concatenate([high, high, low], axis=1),
        jnp.concatenate([applied_ref[...], applied_ref[:k_dim]], axis=0),
        preferred_element_type=F32,
    )


def swap(x, axis, mask):
    size = lax.axis_size(axis)
    return lax.ppermute(x, axis, [(i, i ^ mask) for i in range(size)])


def bits(axis):
    return [1 << i for i in range(lax.axis_size(axis).bit_length() - 1)]


def body(subspace, tiles, tile_count, tile_slot, fetch_list):
    k_dim, row_count = subspace.shape
    blocks, slots, rows, cols = tiles.shape
    peers = lax.axis_size("dev")
    cap = fetch_list.shape[2]
    chips = peers // 2
    me = lax.axis_index("dev").astype(jnp.int32).reshape(1)

    lists = fetch_list.reshape(1, peers * cap)
    for mask in bits("dev"):
        lists = jnp.concatenate([lists, swap(lists, "dev", mask)], axis=0)

    scaled, inv_root = pl.pallas_call(
        degree_kernel,
        out_shape=(
            jax.ShapeDtypeStruct((blocks, k_dim, cols), BF16),
            jax.ShapeDtypeStruct((8, row_count), F32),
        ),
        in_specs=[SMEM, VMEM, VMEM],
        out_specs=(VMEM, VMEM),
        compiler_params=limit(12),
        cost_estimate=pl.CostEstimate(
            flops=16 * tiles.size, bytes_accessed=2 * tiles.size, transcendentals=0
        ),
        name="degree",
    )(tile_count, tiles, subspace)

    sends = pl.pallas_call(
        select_kernel,
        out_shape=[jax.ShapeDtypeStruct((2, cap, k_dim, cols), BF16)] * chips,
        in_specs=[SMEM, SMEM, VMEM],
        out_specs=[VMEM] * chips,
        compiler_params=limit(4),
        name="select",
    )(me, lists, scaled)

    own = sends[0]
    near = [swap(sends[i], "dev", 2 * i) for i in range(1, chips)]
    far = swap(jnp.stack([part[1] for part in [own, *near]]), "dev", 1)

    applied, gram = pl.pallas_call(
        product_kernel,
        out_shape=(
            jax.ShapeDtypeStruct((2 * k_dim, row_count), BF16),
            jax.ShapeDtypeStruct((k_dim // 2, 2 * k_dim), F32),
        ),
        in_specs=[SMEM, SMEM, SMEM] + [VMEM] * (chips + 3),
        out_specs=(VMEM, VMEM),
        scratch_shapes=[pltpu.VMEM((peers * cap, k_dim, cols), BF16)],
        compiler_params=limit(16),
        cost_estimate=pl.CostEstimate(
            flops=2 * tiles.size * k_dim, bytes_accessed=2 * tiles.size, transcendentals=0
        ),
        name="product",
    )(me, tile_count, tile_slot, inv_root, tiles, own, *near, far)

    stages = [("dev", mask) for mask in bits("dev")] + [("grp", mask) for mask in bits("grp")]
    for axis, mask in stages[:-1]:
        gram = gram + swap(gram, axis, mask)
    other = swap(gram, *stages[-1])

    return pl.pallas_call(
        solve_kernel,
        out_shape=jax.ShapeDtypeStruct((k_dim, row_count), F32),
        in_specs=[VMEM] * 3,
        out_specs=VMEM,
        compiler_params=limit(4),
        name="solve",
    )(gram, other, applied)


def solution(mesh):
    placed = (
        P(None, ("grp", "dev")),
        P(("grp", "dev"), None, None, None),
        P(("grp", "dev")),
        P(("grp", "dev"), None),
        P(("grp", "dev"), None, None),
    )
    return jax.shard_map(
        body, mesh=mesh, in_specs=placed, out_specs=P(None, ("grp", "dev")), check_vma=False
    )
```

```python
import jax
import jax.numpy as jnp
from jax import lax
from jax.experimental import pallas as pl
from jax.experimental.pallas import tpu as pltpu
from jax.sharding import PartitionSpec as P

VMEM = pl.BlockSpec(memory_space=pltpu.VMEM)
SMEM = pl.BlockSpec(memory_space=pltpu.SMEM)
NT = (((1,), (1,)), ((), ()))
F32 = jnp.float32
BF16 = jnp.bfloat16


def limit(mib):
    return pltpu.CompilerParams(vmem_limit_bytes=mib << 20)


def split(x):
    high = x.astype(BF16)
    return high, (x - high.astype(F32)).astype(BF16)


def start_kernel(out_ref):
    out_ref[...] = jnp.zeros_like(out_ref)


def degree_kernel(first_ref, count_ref, tiles_ref, inv_ref):
    blocks, slots, rows, cols = tiles_ref.shape
    ones = jnp.ones((8, 2 * cols), BF16)
    slot_of_lane = lax.broadcasted_iota(jnp.int32, (8, slots * cols), 1) // cols
    for b in range(blocks):
        count = count_ref[b]
        tiles = [tiles_ref[b, t] for t in range(slots)]
        if b % 2:
            total = sum(
                tile.astype(F32) * jnp.where(t < count, 1.0, 0.0) for t, tile in enumerate(tiles)
            )
            live, row = ones, split(total)
        else:
            live = (slot_of_lane < count).astype(F32).astype(BF16)
            row = tiles
        degree = lax.dot_general(
            live, jnp.concatenate(row, axis=1), NT, preferred_element_type=F32
        )
        inv_ref[b : b + 1] = lax.rsqrt(degree[:1])


def select_kernel(*refs):
    chips = (len(refs) - 4) // 2
    list_refs, (sub_ref, sib_sub_ref, inv_ref, sib_inv_ref), send_refs = (
        refs[:chips],
        refs[chips : chips + 4],
        refs[chips + 4 :],
    )
    cap, cols = list_refs[0].shape[1], inv_ref.shape[1]
    me = lax.axis_index("dev")
    sources = ((me, sub_ref, inv_ref), (me ^ 1, sib_sub_ref, sib_inv_ref))
    for wanted, send in zip(list_refs, send_refs, strict=True):
        for core, (source, columns, inv) in enumerate(sources):
            for j in range(cap):
                block = wanted[0, j, source]
                lanes = pl.ds(pl.multiple_of(block * cols, cols), cols)
                scaled = columns[:, lanes].astype(F32) * inv[pl.ds(block, 1), :]
                send[core, j] = scaled.astype(BF16)


def product_kernel(count_ref, slot_ref, inv_ref, tiles_ref, *refs):
    *part_refs, applied_ref, gram_ref, table = refs
    blocks, slots, rows, cols = tiles_ref.shape
    _, cap, k_dim, _ = part_refs[0].shape
    me = lax.axis_index("dev")
    dead = table.shape[0] - 1
    table[dead] = jnp.zeros((k_dim, cols), BF16)
    for i, part in enumerate(part_refs):
        for core in range(2):
            for j in range(cap):
                table[((2 * i + core) ^ me) * cap + j] = part[core, j]
    for b in range(blocks):
        count = count_ref[b]
        parts = [table[jnp.where(t < count, slot_ref[b, t], dead)] for t in range(slots)]
        total = lax.dot_general(
            jnp.concatenate(parts, axis=1),
            jnp.concatenate([tiles_ref[b, t] for t in range(slots)], axis=1),
            NT,
            preferred_element_type=F32,
        )
        lanes = slice(b * rows, (b + 1) * rows)
        high, low = split(total * inv_ref[b : b + 1])
        applied_ref[:k_dim, lanes] = high
        applied_ref[k_dim:, lanes] = low
    both = applied_ref[...]
    wide = lax.dot_general(both, both, NT, preferred_element_type=F32)
    wide = wide[:k_dim] + wide[k_dim:]
    gram = wide[:, :k_dim] + wide[:, k_dim:]
    half = k_dim // 2
    gram_ref[...] = jnp.concatenate([gram[:half], gram[half:]], axis=1)


def inverse_factor(gram):
    k_dim = gram.shape[0]
    wide, groups = 2 * k_dim, k_dim // 8
    square = (k_dim, k_dim)
    eye = (
        lax.broadcasted_iota(jnp.int32, square, 0) == lax.broadcasted_iota(jnp.int32, square, 1)
    ).astype(F32)
    diagonal = gram * eye
    row_scale = lax.rsqrt(jnp.sum(diagonal, axis=1, keepdims=True))
    col_scale = lax.rsqrt(jnp.sum(diagonal, axis=0, keepdims=True))
    whole = jnp.concatenate([gram * row_scale * col_scale, eye * col_scale], axis=1)
    rows = [whole[8 * i : 8 * i + 8] for i in range(groups)]
    row_ids = lax.broadcasted_iota(jnp.int32, (8, wide), 0)

    def spread(x):
        return jnp.broadcast_to(x, (8, wide))

    done = []
    for g in range(groups):
        column = {
            (i, b): spread(rows[i][:, 8 * g + b : 8 * g + b + 1])
            for i in range(g, groups)
            for b in range(8)
        }
        out = rows[g]
        for s in range(0, 8, 2):
            row0, row1 = spread(rows[g][s : s + 1]), spread(rows[g][s + 1 : s + 2])
            pivot0 = {b: spread(column[g, b][s : s + 1]) for b in range(s, 8)}
            pivot1 = {b: spread(column[g, b][s + 1 : s + 2]) for b in range(s, 8)}
            p00, p01, p11 = pivot0[s], pivot0[s + 1], pivot1[s + 1]
            det = p00 * p11 - p01 * p01
            inv_det = pl.reciprocal(det, approx=True)
            inv_det = inv_det * (2.0 - det * inv_det)
            q00, q01, q11 = p11 * inv_det, p01 * inv_det, p00 * inv_det
            root0 = lax.rsqrt(p00)
            ratio = p01 * (root0 * root0)
            root1 = lax.rsqrt(p11 - p01 * ratio)
            out = jnp.where(row_ids == s, row0 * root0, out)
            out = jnp.where(row_ids == s + 1, (row1 - ratio * row0) * root1, out)
            for i in range(g, groups):
                x, y = column[i, s], column[i, s + 1]
                f0, f1 = q00 * x - q01 * y, q11 * y - q01 * x
                if i == g:
                    f0 = jnp.where(row_ids > s + 1, f0, 0.0)
                    f1 = jnp.where(row_ids > s + 1, f1, 0.0)
                rows[i] = rows[i] - f0 * row0 - f1 * row1
                for b in range(s + 2, 8):
                    column[i, b] = column[i, b] - f0 * pivot0[b] - f1 * pivot1[b]
        done.append(out)
    return jnp.concatenate(done, axis=0)[:, k_dim:]


def solve_kernel(gram_ref, applied_ref, out_ref):
    k_dim = gram_ref.shape[1] // 2
    packed = gram_ref[...]
    gram = jnp.concatenate([packed[:, :k_dim], packed[:, k_dim:]], axis=0)
    high, low = split(inverse_factor(gram))
    out_ref[...] = jnp.dot(
        jnp.concatenate([high, high, low], axis=1),
        jnp.concatenate([applied_ref[...], applied_ref[:k_dim]], axis=0),
        preferred_element_type=F32,
    )


def swap(x, axis, mask, odd_mask=None):
    odd = mask if odd_mask is None else odd_mask
    size = lax.axis_size(axis)
    core = lax.axis_size("dev") if axis != "dev" else 1
    if odd_mask is None or axis == "dev":
        return lax.ppermute(x, axis, [(i, i ^ (odd if i % 2 else mask)) for i in range(size)])
    pairs = [(i, i ^ (core * (odd if i % 2 else mask))) for i in range(size * core)]
    return lax.ppermute(x, (axis, "dev"), pairs)


def stages(axis):
    masks = [1 << i for i in range(axis == "dev", lax.axis_size(axis).bit_length() - 1)]
    return [masks[i : i + 2] for i in range(0, len(masks), 2)]


def sum_all(x):
    x = x + swap(x, "dev", 1)
    for axis in ("dev", "grp"):
        for masks in stages(axis):
            if len(masks) == 1:
                parts = [swap(x, axis, masks[0])]
            else:
                mine = swap(x, axis, *masks)
                both = swap(x, axis, masks[0] ^ masks[1])
                parts = [mine, both, swap(mine, "dev", 1)]
            x = x + sum(parts)
    return x


def body(subspace, tiles, tile_count, tile_slot, fetch_list):
    k_dim, row_count = subspace.shape
    blocks, slots, rows, cols = tiles.shape
    peers = lax.axis_size("dev")
    cap = fetch_list.shape[2]
    chips = peers // 2
    first = pl.pallas_call(
        start_kernel,
        out_shape=jax.ShapeDtypeStruct((8, 128), F32),
        out_specs=VMEM,
        compiler_params=limit(1),
        cost_estimate=pl.CostEstimate(flops=10**10, bytes_accessed=0, transcendentals=0),
        name="start",
    )()
    first, lists = lax.optimization_barrier((first, jnp.transpose(fetch_list, (0, 2, 1))))
    lists = [lists] + [swap(lists, "dev", 2 * i) for i in range(1, chips)]
    sib_columns = swap(subspace, "dev", 1)

    inv_root = pl.pallas_call(
        degree_kernel,
        out_shape=jax.ShapeDtypeStruct((blocks, rows), F32),
        in_specs=[VMEM, SMEM, VMEM],
        out_specs=VMEM,
        compiler_params=limit(4),
        cost_estimate=pl.CostEstimate(
            flops=16 * tiles.size, bytes_accessed=2 * tiles.size, transcendentals=0
        ),
        name="degree",
    )(first, tile_count, tiles)
    inv_root, *lists = lax.optimization_barrier((inv_root, *lists))
    sib_inv_root = swap(inv_root, "dev", 1)

    sends = pl.pallas_call(
        select_kernel,
        out_shape=[jax.ShapeDtypeStruct((2, cap, k_dim, cols), BF16)] * chips,
        in_specs=[SMEM] * chips + [VMEM] * 4,
        out_specs=[VMEM] * chips,
        compiler_params=limit(2),
        name="select",
    )(*lists, subspace, sib_columns, inv_root, sib_inv_root)
    parts = [sends[0]] + [swap(sends[i], "dev", 2 * i) for i in range(1, chips)]

    applied, gram = pl.pallas_call(
        product_kernel,
        out_shape=(
            jax.ShapeDtypeStruct((2 * k_dim, row_count), BF16),
            jax.ShapeDtypeStruct((k_dim // 2, 2 * k_dim), F32),
        ),
        in_specs=[SMEM, SMEM] + [VMEM] * (chips + 2),
        out_specs=(VMEM, VMEM),
        scratch_shapes=[pltpu.VMEM((peers * cap + 1, k_dim, cols), BF16)],
        compiler_params=limit(4),
        cost_estimate=pl.CostEstimate(
            flops=2 * tiles.size * k_dim, bytes_accessed=2 * tiles.size, transcendentals=0
        ),
        name="product",
    )(tile_count, tile_slot, inv_root, tiles, *parts)

    gram = sum_all(gram)

    return pl.pallas_call(
        solve_kernel,
        out_shape=jax.ShapeDtypeStruct((k_dim, row_count), F32),
        in_specs=[VMEM] * 2,
        out_specs=VMEM,
        compiler_params=limit(4),
        name="solve",
    )(gram, applied)


def solution(mesh):
    placed = (
        P(None, ("grp", "dev")),
        P(("grp", "dev"), None, None, None),
        P(("grp", "dev")),
        P(("grp", "dev"), None),
        P(("grp", "dev"), None, None),
    )
    return jax.shard_map(
        body, mesh=mesh, in_specs=placed, out_specs=P(None, ("grp", "dev")), check_vma=False
    )
```

```python
import functools

import jax
import jax.numpy as jnp
from jax import lax
from jax.experimental import pallas as pl
from jax.experimental.pallas import tpu as pltpu
from jax.sharding import PartitionSpec as P

GROUP = 4
VMEM = pl.BlockSpec(memory_space=pltpu.VMEM)
HBM = pl.BlockSpec(memory_space=pltpu.HBM)
SMEM = pl.BlockSpec(memory_space=pltpu.SMEM)
NT = (((1,), (1,)), ((), ()))
F32 = jnp.float32
BF16 = jnp.bfloat16


def limit(mib):
    return pltpu.CompilerParams(vmem_limit_bytes=mib << 20)


def split(x):
    high = x.astype(BF16)
    return high, (x - high.astype(F32)).astype(BF16)


def start_kernel(out_ref):
    out_ref[...] = jnp.zeros_like(out_ref)


def degree_kernel(first_ref, count_ref, tiles_ref, inv_ref):
    blocks, slots, rows, cols = tiles_ref.shape
    ones = jnp.ones((8, 2 * cols), BF16)
    slot_of_lane = lax.broadcasted_iota(jnp.int32, (8, slots * cols), 1) // cols
    for b in range(blocks):
        count = count_ref[:, b : b + 1]
        tiles = [tiles_ref[b, t] for t in range(slots)]
        if b % 2:
            total = sum(
                tile.astype(F32) * (t < count).astype(F32) for t, tile in enumerate(tiles)
            )
            live, row = ones, split(total)
        else:
            live = (slot_of_lane < count).astype(F32).astype(BF16)
            row = tiles
        degree = lax.dot_general(
            live, jnp.concatenate(row, axis=1), NT, preferred_element_type=F32
        )
        inv_ref[b : b + 1] = lax.rsqrt(degree[:1])


def join_kernel(*refs):
    *list_refs, out_ref, sems = refs
    copies = [
        pltpu.make_async_copy(ref.at[0], out_ref.at[i], sems.at[i]) for i, ref in enumerate(list_refs)
    ]
    for copy in copies:
        copy.start()
    for copy in copies:
        copy.wait()


def select_kernel(masks, lists_ref, sub_ref, sib_sub_ref, inv_ref, sib_inv_ref, *send_refs):
    cap, cols = lists_ref.shape[1], inv_ref.shape[1]
    me = lax.axis_index("dev")
    sources = ((me, sub_ref, inv_ref), (me ^ 1, sib_sub_ref, sib_inv_ref))
    ids = [
        [lists_ref[mask // 2, j, source] for source, _, _ in sources for j in range(cap)]
        for mask in masks
    ]
    for blocks, send in zip(ids, send_refs, strict=True):
        scaled = []
        for i, block in enumerate(blocks):
            _, columns, inv = sources[i // cap]
            lanes = pl.ds(pl.multiple_of(block * cols, cols), cols)
            scaled.append(columns[:, lanes].astype(F32) * inv[pl.ds(block, 1), :])
        for i, block in enumerate(scaled):
            send[i // cap, i % cap] = block.astype(BF16)


def plan_kernel(count_hbm, slot_hbm, count_ref, slot_ref, sems):
    copies = [
        pltpu.make_async_copy(count_hbm, count_ref, sems.at[0]),
        pltpu.make_async_copy(slot_hbm, slot_ref, sems.at[1]),
    ]
    for copy in copies:
        copy.start()
    for copy in copies:
        copy.wait()


def product_kernel(masks, count_ref, slot_ref, inv_ref, tiles_ref, *refs):
    *part_refs, applied_ref, gram_ref, table = refs
    blocks, slots, rows, cols = tiles_ref.shape
    _, cap, k_dim, _ = part_refs[0].shape
    me = lax.axis_index("dev")
    dead = table.shape[0] - 1
    table[dead] = jnp.zeros((k_dim, cols), BF16)
    for mask, part in zip(masks, part_refs, strict=True):
        for core in range(2):
            for j in range(cap):
                table[((mask + core) ^ me) * cap + j] = part[core, j]
    for first in range(0, blocks, GROUP):
        group = range(first, first + GROUP)
        parts, tiles = [], []
        for b in group:
            count = count_ref[b]
            entries = [jnp.where(t < count, slot_ref[b, t], dead) for t in range(slots)]
            parts.append(jnp.concatenate([table[entry] for entry in entries], axis=1))
            tiles.append(jnp.concatenate([tiles_ref[b, t] for t in range(slots)], axis=1))
        total = lax.dot_general(
            jnp.concatenate(parts, axis=0),
            jnp.concatenate(tiles, axis=0),
            NT,
            preferred_element_type=F32,
        )
        for i, b in enumerate(group):
            lanes = slice(b * rows, (b + 1) * rows)
            own = total[i * k_dim : (i + 1) * k_dim, i * rows : (i + 1) * rows]
            high, low = split(own * inv_ref[b : b + 1])
            applied_ref[:k_dim, lanes] = high
            applied_ref[k_dim:, lanes] = low
    both = applied_ref[...]
    wide = lax.dot_general(both, both, NT, preferred_element_type=F32)
    wide = wide[:k_dim] + wide[k_dim:]
    gram = wide[:, :k_dim] + wide[:, k_dim:]
    half = k_dim // 2
    gram_ref[...] = jnp.concatenate([gram[:half], gram[half:]], axis=1)


def inverse_factor(gram):
    k_dim = gram.shape[0]
    wide, groups = 2 * k_dim, k_dim // 8
    square = (k_dim, k_dim)
    eye = (
        lax.broadcasted_iota(jnp.int32, square, 0) == lax.broadcasted_iota(jnp.int32, square, 1)
    ).astype(F32)
    diagonal = gram * eye
    row_scale = lax.rsqrt(jnp.sum(diagonal, axis=1, keepdims=True))
    col_scale = lax.rsqrt(jnp.sum(diagonal, axis=0, keepdims=True))
    whole = jnp.concatenate([gram * row_scale * col_scale, eye * col_scale], axis=1)
    rows = [whole[8 * i : 8 * i + 8] for i in range(groups)]
    row_ids = lax.broadcasted_iota(jnp.int32, (8, wide), 0)

    def spread(x):
        return jnp.broadcast_to(x, (8, wide))

    done = []
    for g in range(groups):
        column = {
            (i, b): spread(rows[i][:, 8 * g + b : 8 * g + b + 1])
            for i in range(g, groups)
            for b in range(8)
        }
        out = rows[g]
        for s in range(0, 8, 2):
            row0, row1 = spread(rows[g][s : s + 1]), spread(rows[g][s + 1 : s + 2])
            pivot0 = {b: spread(column[g, b][s : s + 1]) for b in range(s, 8)}
            pivot1 = {b: spread(column[g, b][s + 1 : s + 2]) for b in range(s, 8)}
            p00, p01, p11 = pivot0[s], pivot0[s + 1], pivot1[s + 1]
            det = p00 * p11 - p01 * p01
            inv_det = pl.reciprocal(det, approx=True)
            inv_det = inv_det * (2.0 - det * inv_det)
            q00, q01, q11 = p11 * inv_det, p01 * inv_det, p00 * inv_det
            root0 = lax.rsqrt(p00)
            ratio = p01 * (root0 * root0)
            root1 = lax.rsqrt(p11 - p01 * ratio)
            out = jnp.where(row_ids == s, row0 * root0, out)
            out = jnp.where(row_ids == s + 1, (row1 - ratio * row0) * root1, out)
            for i in range(g, groups):
                x, y = column[i, s], column[i, s + 1]
                f0, f1 = q00 * x - q01 * y, q11 * y - q01 * x
                if i == g:
                    f0 = jnp.where(row_ids > s + 1, f0, 0.0)
                    f1 = jnp.where(row_ids > s + 1, f1, 0.0)
                rows[i] = rows[i] - f0 * row0 - f1 * row1
                for b in range(s + 2, 8):
                    column[i, b] = column[i, b] - f0 * pivot0[b] - f1 * pivot1[b]
        done.append(out)
    return jnp.concatenate(done, axis=0)[:, k_dim:]


def solve_kernel(gram_ref, applied_ref, out_ref):
    k_dim = gram_ref.shape[1] // 2
    packed = gram_ref[...]
    gram = jnp.concatenate([packed[:, :k_dim], packed[:, k_dim:]], axis=0)
    high, low = split(inverse_factor(gram))
    out_ref[...] = jnp.dot(
        jnp.concatenate([high, high, low], axis=1),
        jnp.concatenate([applied_ref[...], applied_ref[:k_dim]], axis=0),
        preferred_element_type=F32,
    )


def swap(x, axis, mask, odd_mask=None):
    odd = mask if odd_mask is None else odd_mask
    size = lax.axis_size(axis)
    core = lax.axis_size("dev") if axis != "dev" else 1
    if odd_mask is None or axis == "dev":
        return lax.ppermute(x, axis, [(i, i ^ (odd if i % 2 else mask)) for i in range(size)])
    pairs = [(i, i ^ (core * (odd if i % 2 else mask))) for i in range(size * core)]
    return lax.ppermute(x, (axis, "dev"), pairs)


def stages(axis):
    masks = [1 << i for i in range(axis == "dev", lax.axis_size(axis).bit_length() - 1)]
    return [masks[i : i + 2] for i in range(0, len(masks), 2)]


def sum_all(x):
    x = x + swap(x, "dev", 1)
    for axis in ("dev", "grp"):
        for masks in stages(axis):
            if len(masks) == 1:
                parts = [swap(x, axis, masks[0])]
            else:
                mine = swap(x, axis, *masks)
                both = swap(x, axis, masks[0] ^ masks[1])
                parts = [mine, both, swap(mine, "dev", 1)]
            x = x + sum(parts)
    return x


def body(subspace, tiles, tile_count, tile_slot, fetch_list):
    k_dim, row_count = subspace.shape
    blocks, slots, rows, cols = tiles.shape
    peers = lax.axis_size("dev")
    cap = fetch_list.shape[2]
    chips = peers // 2
    first = pl.pallas_call(
        start_kernel,
        out_shape=jax.ShapeDtypeStruct((8, 128), F32),
        out_specs=VMEM,
        compiler_params=limit(1),
        cost_estimate=pl.CostEstimate(flops=10**10, bytes_accessed=0, transcendentals=0),
        name="start",
    )()
    first, lists = lax.optimization_barrier((first, jnp.transpose(fetch_list, (0, 2, 1))))
    masks = [0] + [2 * i for i in reversed(range(1, chips))]
    lists = [lists] + [swap(lists, "dev", 2 * i) for i in range(1, chips)]
    sib_columns = swap(subspace, "dev", 1)

    inv_root = pl.pallas_call(
        degree_kernel,
        out_shape=jax.ShapeDtypeStruct((blocks, rows), F32),
        in_specs=[VMEM] * 3,
        out_specs=VMEM,
        compiler_params=limit(4),
        cost_estimate=pl.CostEstimate(
            flops=16 * tiles.size, bytes_accessed=2 * tiles.size, transcendentals=0
        ),
        name="degree",
    )(first, tile_count.reshape(1, blocks), tiles)
    sib_inv_root = swap(inv_root, "dev", 1)
    lists = pl.pallas_call(
        join_kernel,
        out_shape=pltpu.SMEM((chips, cap, peers), jnp.int32),
        in_specs=[VMEM] * chips,
        out_specs=SMEM,
        scratch_shapes=[pltpu.SemaphoreType.DMA((chips,))],
        compiler_params=limit(1),
        cost_estimate=pl.CostEstimate(flops=2 * 10**9, bytes_accessed=0, transcendentals=0),
        name="join",
    )(*lists)
    sends = pl.pallas_call(
        functools.partial(select_kernel, masks),
        out_shape=[jax.ShapeDtypeStruct((2, cap, k_dim, cols), BF16)] * chips,
        in_specs=[SMEM] + [VMEM] * 4,
        out_specs=[VMEM] * chips,
        compiler_params=limit(2),
        name="select",
    )(pltpu.with_memory_space_constraint(lists, pltpu.SMEM), subspace, sib_columns, inv_root, sib_inv_root)
    parts = [swap(x, "dev", mask) if mask else x for x, mask in zip(sends, masks, strict=True)]

    plan = pl.pallas_call(
        plan_kernel,
        out_shape=[pltpu.SMEM(x.shape, x.dtype) for x in (tile_count, tile_slot)],
        in_specs=[HBM] * 2,
        out_specs=[SMEM] * 2,
        scratch_shapes=[pltpu.SemaphoreType.DMA((2,))],
        compiler_params=limit(1),
        cost_estimate=pl.CostEstimate(flops=2 * 10**9, bytes_accessed=0, transcendentals=0),
        name="plan",
    )(*(pltpu.with_memory_space_constraint(x, pltpu.HBM) for x in (tile_count, tile_slot)))
    plan = [pltpu.with_memory_space_constraint(x, pltpu.SMEM) for x in plan]

    applied, gram = pl.pallas_call(
        functools.partial(product_kernel, masks),
        out_shape=(
            jax.ShapeDtypeStruct((2 * k_dim, row_count), BF16),
            jax.ShapeDtypeStruct((k_dim // 2, 2 * k_dim), F32),
        ),
        in_specs=[SMEM, SMEM] + [VMEM] * (chips + 2),
        out_specs=(VMEM, VMEM),
        scratch_shapes=[pltpu.VMEM((peers * cap + 1, k_dim, cols), BF16)],
        compiler_params=limit(4),
        cost_estimate=pl.CostEstimate(
            flops=2 * tiles.size * k_dim, bytes_accessed=2 * tiles.size, transcendentals=0
        ),
        name="product",
    )(*plan, inv_root, tiles, *parts)

    gram = sum_all(gram)

    return pl.pallas_call(
        solve_kernel,
        out_shape=jax.ShapeDtypeStruct((k_dim, row_count), F32),
        in_specs=[VMEM] * 2,
        out_specs=VMEM,
        compiler_params=limit(4),
        name="solve",
    )(gram, applied)


def solution(mesh):
    placed = (
        P(None, ("grp", "dev")),
        P(("grp", "dev"), None, None, None),
        P(("grp", "dev")),
        P(("grp", "dev"), None),
        P(("grp", "dev"), None, None),
    )
    return jax.shard_map(
        body, mesh=mesh, in_specs=placed, out_specs=P(None, ("grp", "dev")), check_vma=False
    )
```

```python
import functools

import jax
import jax.numpy as jnp
from jax import lax
from jax.experimental import pallas as pl
from jax.experimental.pallas import tpu as pltpu
from jax.sharding import PartitionSpec as P

GROUP = 4
VMEM = pl.BlockSpec(memory_space=pltpu.VMEM)
HBM = pl.BlockSpec(memory_space=pltpu.HBM)
SMEM = pl.BlockSpec(memory_space=pltpu.SMEM)
NT = (((1,), (1,)), ((), ()))
F32 = jnp.float32
BF16 = jnp.bfloat16


def limit(mib):
    return pltpu.CompilerParams(vmem_limit_bytes=mib << 20)


def split(x):
    high = x.astype(BF16)
    return high, (x - high.astype(F32)).astype(BF16)


def start_kernel(out_ref):
    out_ref[...] = jnp.zeros_like(out_ref)


def degree_kernel(first_ref, count_ref, tiles_ref, inv_ref):
    blocks, slots, rows, cols = tiles_ref.shape
    ones = jnp.ones((8, 2 * cols), BF16)
    slot_of_lane = lax.broadcasted_iota(jnp.int32, (8, slots * cols), 1) // cols
    for b in range(blocks):
        count = count_ref[:, b : b + 1]
        tiles = [tiles_ref[b, t] for t in range(slots)]
        if b % 2:
            total = sum(
                tile.astype(F32) * (t < count).astype(F32) for t, tile in enumerate(tiles)
            )
            live, row = ones, split(total)
        else:
            live = (slot_of_lane < count).astype(F32).astype(BF16)
            row = tiles
        degree = lax.dot_general(
            live, jnp.concatenate(row, axis=1), NT, preferred_element_type=F32
        )
        inv_ref[b : b + 1] = lax.rsqrt(degree[:1])


def join_kernel(*refs):
    *list_refs, out_ref, sems = refs
    copies = [
        pltpu.make_async_copy(ref.at[0], out_ref.at[i], sems.at[i]) for i, ref in enumerate(list_refs)
    ]
    for copy in copies:
        copy.start()
    for copy in copies:
        copy.wait()


def select_kernel(masks, lists_ref, sub_ref, sib_sub_ref, inv_ref, sib_inv_ref, *send_refs):
    cap, cols = lists_ref.shape[1], inv_ref.shape[1]
    me = lax.axis_index("dev")
    sources = ((me, sub_ref, inv_ref), (me ^ 1, sib_sub_ref, sib_inv_ref))
    ids = [
        [lists_ref[mask // 2, j, source] for source, _, _ in sources for j in range(cap)]
        for mask in masks
    ]
    for blocks, send in zip(ids, send_refs, strict=True):
        scaled = []
        for i, block in enumerate(blocks):
            _, columns, inv = sources[i // cap]
            lanes = pl.ds(pl.multiple_of(block * cols, cols), cols)
            scaled.append(columns[:, lanes].astype(F32) * inv[pl.ds(block, 1), :])
        for i, block in enumerate(scaled):
            send[i // cap, i % cap] = block.astype(BF16)


def plan_kernel(count_hbm, slot_hbm, count_ref, slot_ref, sems):
    copies = [
        pltpu.make_async_copy(count_hbm, count_ref, sems.at[0]),
        pltpu.make_async_copy(slot_hbm, slot_ref, sems.at[1]),
    ]
    for copy in copies:
        copy.start()
    for copy in copies:
        copy.wait()


def product_kernel(masks, count_ref, slot_ref, inv_ref, tiles_ref, *refs):
    *part_refs, applied_ref, gram_ref, table = refs
    blocks, slots, rows, cols = tiles_ref.shape
    _, cap, k_dim, _ = part_refs[0].shape
    me = lax.axis_index("dev")
    dead = table.shape[0] - 1
    table[dead] = jnp.zeros((k_dim, cols), BF16)
    for mask, part in zip(masks, part_refs, strict=True):
        for core in range(2):
            for j in range(cap):
                table[((mask + core) ^ me) * cap + j] = part[core, j]
    for first in range(0, blocks, GROUP):
        group = range(first, first + GROUP)
        parts, tiles = [], []
        for b in group:
            count = count_ref[b]
            entries = [jnp.where(t < count, slot_ref[b, t], dead) for t in range(slots)]
            parts.append(jnp.concatenate([table[entry] for entry in entries], axis=1))
            tiles.append(jnp.concatenate([tiles_ref[b, t] for t in range(slots)], axis=1))
        total = lax.dot_general(
            jnp.concatenate(parts, axis=0),
            jnp.concatenate(tiles, axis=0),
            NT,
            preferred_element_type=F32,
        )
        for i, b in enumerate(group):
            lanes = slice(b * rows, (b + 1) * rows)
            own = total[i * k_dim : (i + 1) * k_dim, i * rows : (i + 1) * rows]
            high, low = split(own * inv_ref[b : b + 1])
            applied_ref[:k_dim, lanes] = high
            applied_ref[k_dim:, lanes] = low
    both = applied_ref[...]
    wide = lax.dot_general(both, both, NT, preferred_element_type=F32)
    wide = wide[:k_dim] + wide[k_dim:]
    gram = wide[:, :k_dim] + wide[:, k_dim:]
    half = k_dim // 2
    gram_ref[...] = jnp.concatenate([gram[:half], gram[half:]], axis=1)


def inverse_factor(gram):
    k_dim = gram.shape[0]
    wide, groups = 2 * k_dim, k_dim // 8
    square = (k_dim, k_dim)
    eye = (
        lax.broadcasted_iota(jnp.int32, square, 0) == lax.broadcasted_iota(jnp.int32, square, 1)
    ).astype(F32)
    diagonal = gram * eye
    row_scale = lax.rsqrt(jnp.sum(diagonal, axis=1, keepdims=True))
    col_scale = lax.rsqrt(jnp.sum(diagonal, axis=0, keepdims=True))
    whole = jnp.concatenate([gram * row_scale * col_scale, eye * col_scale], axis=1)
    rows = [whole[8 * i : 8 * i + 8] for i in range(groups)]
    row_ids = lax.broadcasted_iota(jnp.int32, (8, wide), 0)

    def spread(x):
        return jnp.broadcast_to(x, (8, wide))

    done = []
    for g in range(groups):
        column = {
            (i, b): spread(rows[i][:, 8 * g + b : 8 * g + b + 1])
            for i in range(g, groups)
            for b in range(8)
        }
        out = rows[g]
        for s in range(0, 8, 2):
            row0, row1 = spread(rows[g][s : s + 1]), spread(rows[g][s + 1 : s + 2])
            pivot0 = {b: spread(column[g, b][s : s + 1]) for b in range(s, 8)}
            pivot1 = {b: spread(column[g, b][s + 1 : s + 2]) for b in range(s, 8)}
            p00, p01, p11 = pivot0[s], pivot0[s + 1], pivot1[s + 1]
            det = p00 * p11 - p01 * p01
            inv_det = 1.0 / det
            q00, q01, q11 = p11 * inv_det, p01 * inv_det, p00 * inv_det
            root0 = lax.rsqrt(p00)
            ratio = p01 * (root0 * root0)
            root1 = lax.rsqrt(p11 - p01 * ratio)
            out = jnp.where(row_ids == s, row0 * root0, out)
            out = jnp.where(row_ids == s + 1, (row1 - ratio * row0) * root1, out)
            for i in range(g, groups):
                x, y = column[i, s], column[i, s + 1]
                f0, f1 = q00 * x - q01 * y, q11 * y - q01 * x
                if i == g:
                    f0 = jnp.where(row_ids > s + 1, f0, 0.0)
                    f1 = jnp.where(row_ids > s + 1, f1, 0.0)
                rows[i] = rows[i] - f0 * row0 - f1 * row1
                for b in range(s + 2, 8):
                    column[i, b] = column[i, b] - f0 * pivot0[b] - f1 * pivot1[b]
        done.append(out)
    return jnp.concatenate(done, axis=0)[:, k_dim:]


def solve_kernel(gram_ref, applied_ref, out_ref):
    k_dim = gram_ref.shape[1] // 2
    packed = gram_ref[...]
    gram = jnp.concatenate([packed[:, :k_dim], packed[:, k_dim:]], axis=0)
    high, low = split(inverse_factor(gram))
    out_ref[...] = jnp.dot(
        jnp.concatenate([high, high, low], axis=1),
        jnp.concatenate([applied_ref[...], applied_ref[:k_dim]], axis=0),
        preferred_element_type=F32,
    )


def swap(x, axis, mask, odd_mask=None):
    odd = mask if odd_mask is None else odd_mask
    size = lax.axis_size(axis)
    core = lax.axis_size("dev") if axis != "dev" else 1
    if odd_mask is None or axis == "dev":
        return lax.ppermute(x, axis, [(i, i ^ (odd if i % 2 else mask)) for i in range(size)])
    pairs = [(i, i ^ (core * (odd if i % 2 else mask))) for i in range(size * core)]
    return lax.ppermute(x, (axis, "dev"), pairs)


def stages(axis):
    masks = [1 << i for i in range(axis == "dev", lax.axis_size(axis).bit_length() - 1)]
    return [masks[i : i + 2] for i in range(0, len(masks), 2)]


def sum_all(x):
    x = x + swap(x, "dev", 1)
    for axis in ("dev", "grp"):
        for masks in stages(axis):
            if len(masks) == 1:
                parts = [swap(x, axis, masks[0])]
            else:
                mine = swap(x, axis, masks[0], masks[0] ^ masks[1])
                both = swap(x, axis, masks[1])
                parts = [mine, both, swap(mine, "dev", 1)]
            x = x + sum(parts)
    return x


def body(subspace, tiles, tile_count, tile_slot, fetch_list):
    k_dim, row_count = subspace.shape
    blocks, slots, rows, cols = tiles.shape
    peers = lax.axis_size("dev")
    cap = fetch_list.shape[2]
    chips = peers // 2
    first = pl.pallas_call(
        start_kernel,
        out_shape=jax.ShapeDtypeStruct((8, 128), F32),
        out_specs=VMEM,
        compiler_params=limit(1),
        cost_estimate=pl.CostEstimate(flops=10**10, bytes_accessed=0, transcendentals=0),
        name="start",
    )()
    first, lists = lax.optimization_barrier((first, jnp.transpose(fetch_list, (0, 2, 1))))
    masks = [0] + [2 * i for i in reversed(range(1, chips))]
    lists = [lists] + [swap(lists, "dev", 2 * i) for i in range(1, chips)]
    sib_columns = swap(subspace, "dev", 1)

    inv_root = pl.pallas_call(
        degree_kernel,
        out_shape=jax.ShapeDtypeStruct((blocks, rows), F32),
        in_specs=[VMEM] * 3,
        out_specs=VMEM,
        compiler_params=limit(4),
        cost_estimate=pl.CostEstimate(
            flops=16 * tiles.size, bytes_accessed=2 * tiles.size, transcendentals=0
        ),
        name="degree",
    )(first, tile_count.reshape(1, blocks), tiles)
    sib_inv_root = swap(inv_root, "dev", 1)
    lists = pl.pallas_call(
        join_kernel,
        out_shape=pltpu.SMEM((chips, cap, peers), jnp.int32),
        in_specs=[VMEM] * chips,
        out_specs=SMEM,
        scratch_shapes=[pltpu.SemaphoreType.DMA((chips,))],
        compiler_params=limit(1),
        cost_estimate=pl.CostEstimate(flops=2 * 10**9, bytes_accessed=0, transcendentals=0),
        name="join",
    )(*lists)
    sends = pl.pallas_call(
        functools.partial(select_kernel, masks),
        out_shape=[jax.ShapeDtypeStruct((2, cap, k_dim, cols), BF16)] * chips,
        in_specs=[SMEM] + [VMEM] * 4,
        out_specs=[VMEM] * chips,
        compiler_params=limit(2),
        name="select",
    )(pltpu.with_memory_space_constraint(lists, pltpu.SMEM), subspace, sib_columns, inv_root, sib_inv_root)
    parts = [swap(x, "dev", mask) if mask else x for x, mask in zip(sends, masks, strict=True)]

    plan = pl.pallas_call(
        plan_kernel,
        out_shape=[pltpu.SMEM(x.shape, x.dtype) for x in (tile_count, tile_slot)],
        in_specs=[HBM] * 2,
        out_specs=[SMEM] * 2,
        scratch_shapes=[pltpu.SemaphoreType.DMA((2,))],
        compiler_params=limit(1),
        cost_estimate=pl.CostEstimate(flops=2 * 10**9, bytes_accessed=0, transcendentals=0),
        name="plan",
    )(*(pltpu.with_memory_space_constraint(x, pltpu.HBM) for x in (tile_count, tile_slot)))
    plan = [pltpu.with_memory_space_constraint(x, pltpu.SMEM) for x in plan]

    applied, gram = pl.pallas_call(
        functools.partial(product_kernel, masks),
        out_shape=(
            jax.ShapeDtypeStruct((2 * k_dim, row_count), BF16),
            jax.ShapeDtypeStruct((k_dim // 2, 2 * k_dim), F32),
        ),
        in_specs=[SMEM, SMEM] + [VMEM] * (chips + 2),
        out_specs=(VMEM, VMEM),
        scratch_shapes=[pltpu.VMEM((peers * cap + 1, k_dim, cols), BF16)],
        compiler_params=limit(4),
        cost_estimate=pl.CostEstimate(
            flops=2 * tiles.size * k_dim, bytes_accessed=2 * tiles.size, transcendentals=0
        ),
        name="product",
    )(*plan, inv_root, tiles, *parts)

    gram = sum_all(gram)

    return pl.pallas_call(
        solve_kernel,
        out_shape=jax.ShapeDtypeStruct((k_dim, row_count), F32),
        in_specs=[VMEM] * 2,
        out_specs=VMEM,
        compiler_params=limit(4),
        name="solve",
    )(gram, applied)


def solution(mesh):
    placed = (
        P(None, ("grp", "dev")),
        P(("grp", "dev"), None, None, None),
        P(("grp", "dev")),
        P(("grp", "dev"), None),
        P(("grp", "dev"), None, None),
    )
    return jax.shard_map(
        body, mesh=mesh, in_specs=placed, out_specs=P(None, ("grp", "dev")), check_vma=False
    )
```

```python
import functools

import jax
import jax.numpy as jnp
from jax import lax
from jax.experimental import pallas as pl
from jax.experimental.pallas import tpu as pltpu
from jax.sharding import PartitionSpec as P

GROUP = 4
VMEM = pl.BlockSpec(memory_space=pltpu.VMEM)
HBM = pl.BlockSpec(memory_space=pltpu.HBM)
SMEM = pl.BlockSpec(memory_space=pltpu.SMEM)
NT = (((1,), (1,)), ((), ()))
F32 = jnp.float32
BF16 = jnp.bfloat16


def limit(mib):
    return pltpu.CompilerParams(vmem_limit_bytes=mib << 20)


def split(x):
    high = x.astype(BF16)
    return high, (x - high.astype(F32)).astype(BF16)


def start_kernel(out_ref):
    out_ref[...] = jnp.zeros_like(out_ref)


def degree_kernel(first_ref, count_ref, tiles_ref, inv_ref):
    blocks, slots, rows, cols = tiles_ref.shape
    ones = jnp.ones((8, 2 * cols), BF16)
    slot_of_lane = lax.broadcasted_iota(jnp.int32, (8, slots * cols), 1) // cols
    for b in range(blocks):
        count = count_ref[:, b : b + 1]
        tiles = [tiles_ref[b, t] for t in range(slots)]
        if b % 2:
            total = sum(
                tile.astype(F32) * (t < count).astype(F32) for t, tile in enumerate(tiles)
            )
            live, row = ones, split(total)
        else:
            live = (slot_of_lane < count).astype(F32).astype(BF16)
            row = tiles
        degree = lax.dot_general(
            live, jnp.concatenate(row, axis=1), NT, preferred_element_type=F32
        )
        inv_ref[b : b + 1] = lax.rsqrt(degree[:1])


def join_kernel(*refs):
    for i, ref in enumerate(refs[:-1]):
        refs[-1][i] = ref[0]


def select_kernel(masks, lists_ref, sub_ref, sib_sub_ref, inv_ref, sib_inv_ref, *send_refs):
    cap, cols = lists_ref.shape[1], inv_ref.shape[1]
    me = lax.axis_index("dev")
    sources = ((me, sub_ref, inv_ref), (me ^ 1, sib_sub_ref, sib_inv_ref))
    peer = lax.broadcasted_iota(jnp.int32, (1, lists_ref.shape[2]), 1)

    def block_id(chip, j, source):
        return jnp.sum(jnp.where(peer == source, lists_ref[chip, j : j + 1], 0))

    ids = [
        [block_id(mask // 2, j, source) for source, _, _ in sources for j in range(cap)]
        for mask in masks
    ]
    for blocks, send in zip(ids, send_refs, strict=True):
        scaled = []
        for i, block in enumerate(blocks):
            _, columns, inv = sources[i // cap]
            lanes = pl.ds(pl.multiple_of(block * cols, cols), cols)
            scaled.append(columns[:, lanes].astype(F32) * inv[pl.ds(block, 1), :])
        for i, block in enumerate(scaled):
            send[i // cap, i % cap] = block.astype(BF16)


def plan_kernel(count_hbm, slot_hbm, count_ref, slot_ref, sems):
    copies = [
        pltpu.make_async_copy(count_hbm, count_ref, sems.at[0]),
        pltpu.make_async_copy(slot_hbm, slot_ref, sems.at[1]),
    ]
    for copy in copies:
        copy.start()
    for copy in copies:
        copy.wait()


def product_kernel(masks, count_ref, slot_ref, inv_ref, tiles_ref, *refs):
    *part_refs, applied_ref, gram_ref, table = refs
    blocks, slots, rows, cols = tiles_ref.shape
    _, cap, k_dim, _ = part_refs[0].shape
    me = lax.axis_index("dev")
    dead = table.shape[0] - 1
    table[dead] = jnp.zeros((k_dim, cols), BF16)
    for mask, part in zip(masks, part_refs, strict=True):
        for core in range(2):
            for j in range(cap):
                table[((mask + core) ^ me) * cap + j] = part[core, j]
    for first in range(0, blocks, GROUP):
        group = range(first, first + GROUP)
        parts, tiles = [], []
        for b in group:
            count = count_ref[b]
            entries = [jnp.where(t < count, slot_ref[b, t], dead) for t in range(slots)]
            parts.append(jnp.concatenate([table[entry] for entry in entries], axis=1))
            tiles.append(jnp.concatenate([tiles_ref[b, t] for t in range(slots)], axis=1))
        total = lax.dot_general(
            jnp.concatenate(parts, axis=0),
            jnp.concatenate(tiles, axis=0),
            NT,
            preferred_element_type=F32,
        )
        for i, b in enumerate(group):
            lanes = slice(b * rows, (b + 1) * rows)
            own = total[i * k_dim : (i + 1) * k_dim, i * rows : (i + 1) * rows]
            high, low = split(own * inv_ref[b : b + 1])
            applied_ref[:k_dim, lanes] = high
            applied_ref[k_dim:, lanes] = low
    both = applied_ref[...]
    wide = lax.dot_general(both, both, NT, preferred_element_type=F32)
    wide = wide[:k_dim] + wide[k_dim:]
    gram = wide[:, :k_dim] + wide[:, k_dim:]
    half = k_dim // 2
    gram_ref[...] = jnp.concatenate([gram[:half], gram[half:]], axis=1)


def inverse_factor(gram):
    k_dim = gram.shape[0]
    wide, groups = 2 * k_dim, k_dim // 8
    square = (k_dim, k_dim)
    eye = (
        lax.broadcasted_iota(jnp.int32, square, 0) == lax.broadcasted_iota(jnp.int32, square, 1)
    ).astype(F32)
    diagonal = gram * eye
    row_scale = lax.rsqrt(jnp.sum(diagonal, axis=1, keepdims=True))
    col_scale = lax.rsqrt(jnp.sum(diagonal, axis=0, keepdims=True))
    whole = jnp.concatenate([gram * row_scale * col_scale, eye * col_scale], axis=1)
    rows = [whole[8 * i : 8 * i + 8] for i in range(groups)]
    row_ids = lax.broadcasted_iota(jnp.int32, (8, wide), 0)

    def spread(x):
        return jnp.broadcast_to(x, (8, wide))

    done = []
    for g in range(groups):
        column = {
            (i, b): spread(rows[i][:, 8 * g + b : 8 * g + b + 1])
            for i in range(g, groups)
            for b in range(8)
        }
        out = rows[g]
        for s in range(0, 8, 2):
            row0, row1 = spread(rows[g][s : s + 1]), spread(rows[g][s + 1 : s + 2])
            pivot0 = {b: spread(column[g, b][s : s + 1]) for b in range(s, 8)}
            pivot1 = {b: spread(column[g, b][s + 1 : s + 2]) for b in range(s, 8)}
            p00, p01, p11 = pivot0[s], pivot0[s + 1], pivot1[s + 1]
            det = p00 * p11 - p01 * p01
            inv_det = 1.0 / det
            q00, q01, q11 = p11 * inv_det, p01 * inv_det, p00 * inv_det
            root0 = lax.rsqrt(p00)
            ratio = p01 * (root0 * root0)
            root1 = lax.rsqrt(p11 - p01 * ratio)
            out = jnp.where(row_ids == s, row0 * root0, out)
            out = jnp.where(row_ids == s + 1, (row1 - ratio * row0) * root1, out)
            for i in range(g, groups):
                x, y = column[i, s], column[i, s + 1]
                f0, f1 = q00 * x - q01 * y, q11 * y - q01 * x
                if i == g:
                    f0 = jnp.where(row_ids > s + 1, f0, 0.0)
                    f1 = jnp.where(row_ids > s + 1, f1, 0.0)
                rows[i] = rows[i] - f0 * row0 - f1 * row1
                for b in range(s + 2, 8):
                    column[i, b] = column[i, b] - f0 * pivot0[b] - f1 * pivot1[b]
        done.append(out)
    return jnp.concatenate(done, axis=0)[:, k_dim:]


def solve_kernel(gram_ref, applied_ref, out_ref):
    k_dim = gram_ref.shape[1] // 2
    packed = gram_ref[...]
    gram = jnp.concatenate([packed[:, :k_dim], packed[:, k_dim:]], axis=0)
    high, low = split(inverse_factor(gram))
    out_ref[...] = jnp.dot(
        jnp.concatenate([high, high, low], axis=1),
        jnp.concatenate([applied_ref[...], applied_ref[:k_dim]], axis=0),
        preferred_element_type=F32,
    )


def swap(x, axis, mask, odd_mask=None):
    odd = mask if odd_mask is None else odd_mask
    size = lax.axis_size(axis)
    core = lax.axis_size("dev") if axis != "dev" else 1
    if odd_mask is None or axis == "dev":
        return lax.ppermute(x, axis, [(i, i ^ (odd if i % 2 else mask)) for i in range(size)])
    pairs = [(i, i ^ (core * (odd if i % 2 else mask))) for i in range(size * core)]
    return lax.ppermute(x, (axis, "dev"), pairs)


def stages(axis):
    masks = [1 << i for i in range(axis == "dev", lax.axis_size(axis).bit_length() - 1)]
    return [masks[i : i + 2] for i in range(0, len(masks), 2)]


def sum_all(x):
    x = x + swap(x, "dev", 1)
    for axis in ("dev", "grp"):
        for masks in stages(axis):
            if len(masks) == 1:
                parts = [swap(x, axis, masks[0])]
            else:
                mine = swap(x, axis, masks[0], masks[0] ^ masks[1])
                both = swap(x, axis, masks[1])
                parts = [mine, both, swap(mine, "dev", 1)]
            x = x + sum(parts)
    return x


def body(subspace, tiles, tile_count, tile_slot, fetch_list):
    k_dim, row_count = subspace.shape
    blocks, slots, rows, cols = tiles.shape
    peers = lax.axis_size("dev")
    cap = fetch_list.shape[2]
    chips = peers // 2
    first = pl.pallas_call(
        start_kernel,
        out_shape=jax.ShapeDtypeStruct((8, 128), F32),
        out_specs=VMEM,
        compiler_params=limit(1),
        cost_estimate=pl.CostEstimate(flops=10**10, bytes_accessed=0, transcendentals=0),
        name="start",
    )()
    first, lists = lax.optimization_barrier((first, jnp.transpose(fetch_list, (0, 2, 1))))
    masks = [0] + [2 * i for i in reversed(range(1, chips))]
    lists = [lists] + [swap(lists, "dev", 2 * i) for i in range(1, chips)]
    sib_columns = swap(subspace, "dev", 1)

    inv_root = pl.pallas_call(
        degree_kernel,
        out_shape=jax.ShapeDtypeStruct((blocks, rows), F32),
        in_specs=[VMEM] * 3,
        out_specs=VMEM,
        compiler_params=limit(4),
        cost_estimate=pl.CostEstimate(
            flops=16 * tiles.size, bytes_accessed=2 * tiles.size, transcendentals=0
        ),
        name="degree",
    )(first, tile_count.reshape(1, blocks), tiles)
    sib_inv_root = swap(inv_root, "dev", 1)
    lists = pl.pallas_call(
        join_kernel,
        out_shape=jax.ShapeDtypeStruct((chips, cap, peers), jnp.int32),
        in_specs=[VMEM] * chips,
        out_specs=VMEM,
        compiler_params=limit(1),
        cost_estimate=pl.CostEstimate(flops=2 * 10**9, bytes_accessed=0, transcendentals=0),
        name="join",
    )(*lists)
    sends = pl.pallas_call(
        functools.partial(select_kernel, masks),
        out_shape=[jax.ShapeDtypeStruct((2, cap, k_dim, cols), BF16)] * chips,
        in_specs=[VMEM] * 5,
        out_specs=[VMEM] * chips,
        compiler_params=limit(2),
        name="select",
    )(lists, subspace, sib_columns, inv_root, sib_inv_root)
    parts = [swap(x, "dev", mask) if mask else x for x, mask in zip(sends, masks, strict=True)]

    plan = pl.pallas_call(
        plan_kernel,
        out_shape=[pltpu.SMEM(x.shape, x.dtype) for x in (tile_count, tile_slot)],
        in_specs=[HBM] * 2,
        out_specs=[SMEM] * 2,
        scratch_shapes=[pltpu.SemaphoreType.DMA((2,))],
        compiler_params=limit(1),
        cost_estimate=pl.CostEstimate(flops=2 * 10**9, bytes_accessed=0, transcendentals=0),
        name="plan",
    )(*(pltpu.with_memory_space_constraint(x, pltpu.HBM) for x in (tile_count, tile_slot)))
    plan = [pltpu.with_memory_space_constraint(x, pltpu.SMEM) for x in plan]

    applied, gram = pl.pallas_call(
        functools.partial(product_kernel, masks),
        out_shape=(
            jax.ShapeDtypeStruct((2 * k_dim, row_count), BF16),
            jax.ShapeDtypeStruct((k_dim // 2, 2 * k_dim), F32),
        ),
        in_specs=[SMEM, SMEM] + [VMEM] * (chips + 2),
        out_specs=(VMEM, VMEM),
        scratch_shapes=[pltpu.VMEM((peers * cap + 1, k_dim, cols), BF16)],
        compiler_params=limit(4),
        cost_estimate=pl.CostEstimate(
            flops=2 * tiles.size * k_dim, bytes_accessed=2 * tiles.size, transcendentals=0
        ),
        name="product",
    )(*plan, inv_root, tiles, *parts)

    gram = sum_all(gram)

    return pl.pallas_call(
        solve_kernel,
        out_shape=jax.ShapeDtypeStruct((k_dim, row_count), F32),
        in_specs=[VMEM] * 2,
        out_specs=VMEM,
        compiler_params=limit(4),
        name="solve",
    )(gram, applied)


def solution(mesh):
    placed = (
        P(None, ("grp", "dev")),
        P(("grp", "dev"), None, None, None),
        P(("grp", "dev")),
        P(("grp", "dev"), None),
        P(("grp", "dev"), None, None),
    )
    return jax.shard_map(
        body, mesh=mesh, in_specs=placed, out_specs=P(None, ("grp", "dev")), check_vma=False
    )
```

```python
import functools

import jax
import jax.numpy as jnp
from jax import lax
from jax.experimental import pallas as pl
from jax.experimental.pallas import tpu as pltpu
from jax.sharding import PartitionSpec as P

GROUP = 4
VMEM = pl.BlockSpec(memory_space=pltpu.VMEM)
HBM = pl.BlockSpec(memory_space=pltpu.HBM)
SMEM = pl.BlockSpec(memory_space=pltpu.SMEM)
NT = (((1,), (1,)), ((), ()))
F32 = jnp.float32
BF16 = jnp.bfloat16


def limit(mib):
    return pltpu.CompilerParams(vmem_limit_bytes=mib << 20)


def split(x):
    high = x.astype(BF16)
    return high, (x - high.astype(F32)).astype(BF16)


def start_kernel(out_ref):
    out_ref[...] = jnp.zeros_like(out_ref)


def degree_kernel(first_ref, count_ref, tiles_ref, inv_ref):
    blocks, slots, rows, cols = tiles_ref.shape
    ones = jnp.ones((8, 2 * cols), BF16)
    slot_of_lane = lax.broadcasted_iota(jnp.int32, (8, slots * cols), 1) // cols
    for b in range(blocks):
        count = count_ref[:, b : b + 1]
        tiles = [tiles_ref[b, t] for t in range(slots)]
        if b % 2:
            total = sum(
                tile.astype(F32) * (t < count).astype(F32) for t, tile in enumerate(tiles)
            )
            live, row = ones, split(total)
        else:
            live = (slot_of_lane < count).astype(F32).astype(BF16)
            row = tiles
        degree = lax.dot_general(
            live, jnp.concatenate(row, axis=1), NT, preferred_element_type=F32
        )
        inv_ref[b : b + 1] = lax.rsqrt(degree[:1])


def join_kernel(*refs):
    for i, ref in enumerate(refs[:-1]):
        refs[-1][i] = ref[0]


def select_kernel(masks, lists_ref, sub_ref, sib_sub_ref, inv_ref, sib_inv_ref, *send_refs):
    cap, cols = lists_ref.shape[1], inv_ref.shape[1]
    me = lax.axis_index("dev")
    sources = ((me, sub_ref, inv_ref), (me ^ 1, sib_sub_ref, sib_inv_ref))
    peer = lax.broadcasted_iota(jnp.int32, (1, lists_ref.shape[2]), 1)

    def block_id(chip, j, source):
        return jnp.sum(jnp.where(peer == source, lists_ref[chip, j : j + 1], 0))

    ids = [
        [block_id(mask // 2, j, source) for source, _, _ in sources for j in range(cap)]
        for mask in masks
    ]
    for blocks, send in zip(ids, send_refs, strict=True):
        scaled = []
        for i, block in enumerate(blocks):
            _, columns, inv = sources[i // cap]
            lanes = pl.ds(pl.multiple_of(block * cols, cols), cols)
            scaled.append(columns[:, lanes].astype(F32) * inv[pl.ds(block, 1), :])
        for i, block in enumerate(scaled):
            send[i // cap, i % cap] = block.astype(BF16)


def plan_kernel(count_hbm, slot_hbm, count_ref, slot_ref, sems):
    copies = [
        pltpu.make_async_copy(count_hbm, count_ref, sems.at[0]),
        pltpu.make_async_copy(slot_hbm, slot_ref, sems.at[1]),
    ]
    for copy in copies:
        copy.start()
    for copy in copies:
        copy.wait()


def product_kernel(masks, count_ref, slot_ref, inv_ref, tiles_ref, *refs):
    *part_refs, applied_ref, gram_ref, table = refs
    blocks, slots, rows, cols = tiles_ref.shape
    _, cap, k_dim, _ = part_refs[0].shape
    me = lax.axis_index("dev")
    dead = table.shape[0] - 1
    table[dead] = jnp.zeros((k_dim, cols), BF16)
    for mask, part in zip(masks, part_refs, strict=True):
        for core in range(2):
            for j in range(cap):
                table[((mask + core) ^ me) * cap + j] = part[core, j]
    for first in range(0, blocks, GROUP):
        group = range(first, first + GROUP)
        parts, tiles = [], []
        for b in group:
            count = count_ref[b]
            entries = [jnp.where(t < count, slot_ref[b, t], dead) for t in range(slots)]
            parts.append(jnp.concatenate([table[entry] for entry in entries], axis=1))
            tiles.append(jnp.concatenate([tiles_ref[b, t] for t in range(slots)], axis=1))
        total = lax.dot_general(
            jnp.concatenate(parts, axis=0),
            jnp.concatenate(tiles, axis=0),
            NT,
            preferred_element_type=F32,
        )
        for i, b in enumerate(group):
            lanes = slice(b * rows, (b + 1) * rows)
            own = total[i * k_dim : (i + 1) * k_dim, i * rows : (i + 1) * rows]
            high, low = split(own * inv_ref[b : b + 1])
            applied_ref[:k_dim, lanes] = high
            applied_ref[k_dim:, lanes] = low
    both = applied_ref[...]
    wide = lax.dot_general(both, both, NT, preferred_element_type=F32)
    wide = wide[:k_dim] + wide[k_dim:]
    gram = wide[:, :k_dim] + wide[:, k_dim:]
    half = k_dim // 2
    gram_ref[...] = jnp.concatenate([gram[:half], gram[half:]], axis=1)


def inverse_factor(gram):
    k_dim = gram.shape[0]
    wide, groups = 2 * k_dim, k_dim // 8
    square = (k_dim, k_dim)
    eye = (
        lax.broadcasted_iota(jnp.int32, square, 0) == lax.broadcasted_iota(jnp.int32, square, 1)
    ).astype(F32)
    diagonal = gram * eye
    row_scale = lax.rsqrt(jnp.sum(diagonal, axis=1, keepdims=True))
    col_scale = lax.rsqrt(jnp.sum(diagonal, axis=0, keepdims=True))
    whole = jnp.concatenate([gram * row_scale * col_scale, eye * col_scale], axis=1)
    rows = [whole[8 * i : 8 * i + 8] for i in range(groups)]
    row_ids = lax.broadcasted_iota(jnp.int32, (8, wide), 0)

    def spread(x):
        return jnp.broadcast_to(x, (8, wide))

    done = []
    for g in range(groups):
        column = {
            (i, b): spread(rows[i][:, 8 * g + b : 8 * g + b + 1])
            for i in range(g, groups)
            for b in range(8)
        }
        out = rows[g]
        for s in range(0, 8, 2):
            row0, row1 = spread(rows[g][s : s + 1]), spread(rows[g][s + 1 : s + 2])
            pivot0 = {b: spread(column[g, b][s : s + 1]) for b in range(s, 8)}
            pivot1 = {b: spread(column[g, b][s + 1 : s + 2]) for b in range(s, 8)}
            p00, p01, p11 = pivot0[s], pivot0[s + 1], pivot1[s + 1]
            det = p00 * p11 - p01 * p01
            inv_det = 1.0 / det
            q00, q01, q11 = p11 * inv_det, p01 * inv_det, p00 * inv_det
            root0 = lax.rsqrt(p00)
            ratio = p01 * (root0 * root0)
            root1 = lax.rsqrt(p11 - p01 * ratio)
            out = jnp.where(row_ids == s, row0 * root0, out)
            out = jnp.where(row_ids == s + 1, (row1 - ratio * row0) * root1, out)
            for i in range(g, groups):
                x, y = column[i, s], column[i, s + 1]
                f0, f1 = q00 * x - q01 * y, q11 * y - q01 * x
                if i == g:
                    f0 = jnp.where(row_ids > s + 1, f0, 0.0)
                    f1 = jnp.where(row_ids > s + 1, f1, 0.0)
                rows[i] = rows[i] - f0 * row0 - f1 * row1
                for b in range(s + 2, 8):
                    column[i, b] = column[i, b] - f0 * pivot0[b] - f1 * pivot1[b]
        done.append(out)
    return jnp.concatenate(done, axis=0)[:, k_dim:]


def solve_kernel(gram_ref, applied_ref, out_ref):
    k_dim = gram_ref.shape[1] // 2
    packed = gram_ref[...]
    gram = jnp.concatenate([packed[:, :k_dim], packed[:, k_dim:]], axis=0)
    high, low = split(inverse_factor(gram))
    out_ref[...] = jnp.dot(
        jnp.concatenate([high, high, low], axis=1),
        jnp.concatenate([applied_ref[...], applied_ref[:k_dim]], axis=0),
        preferred_element_type=F32,
    )


def swap(x, axis, mask, odd_mask=None):
    odd = mask if odd_mask is None else odd_mask
    size = lax.axis_size(axis)
    core = lax.axis_size("dev") if axis != "dev" else 1
    if odd_mask is None or axis == "dev":
        return lax.ppermute(x, axis, [(i, i ^ (odd if i % 2 else mask)) for i in range(size)])
    pairs = [(i, i ^ (core * (odd if i % 2 else mask))) for i in range(size * core)]
    return lax.ppermute(x, (axis, "dev"), pairs)


def stages(axis):
    masks = [1 << i for i in range(axis == "dev", lax.axis_size(axis).bit_length() - 1)]
    return [masks[i : i + 2] for i in range(0, len(masks), 2)]


def sum_all(x):
    x = x + swap(x, "dev", 1)
    for axis in ("dev", "grp"):
        for masks in stages(axis):
            if len(masks) == 1:
                parts = [swap(x, axis, masks[0])]
            else:
                mine = swap(x, axis, masks[0], masks[0] ^ masks[1])
                both = swap(x, axis, masks[1])
                parts = [mine, both, swap(mine, "dev", 1)]
            x = x + sum(parts)
    return x


def body(subspace, tiles, tile_count, tile_slot, fetch_list):
    k_dim, row_count = subspace.shape
    blocks, slots, rows, cols = tiles.shape
    peers = lax.axis_size("dev")
    cap = fetch_list.shape[2]
    chips = peers // 2
    lists = jnp.transpose(fetch_list, (0, 2, 1))
    masks = [0] + [2 * i for i in reversed(range(1, chips))]
    lists = [lists] + [swap(lists, "dev", 2 * i) for i in range(1, chips)]
    sib_columns = swap(subspace, "dev", 1)

    first = pl.pallas_call(
        start_kernel,
        out_shape=jax.ShapeDtypeStruct((8, 128), F32),
        out_specs=VMEM,
        compiler_params=limit(1),
        cost_estimate=pl.CostEstimate(flops=10**10, bytes_accessed=0, transcendentals=0),
        name="start",
    )()
    inv_root = pl.pallas_call(
        degree_kernel,
        out_shape=jax.ShapeDtypeStruct((blocks, rows), F32),
        in_specs=[VMEM] * 3,
        out_specs=VMEM,
        compiler_params=limit(4),
        cost_estimate=pl.CostEstimate(
            flops=16 * tiles.size, bytes_accessed=2 * tiles.size, transcendentals=0
        ),
        name="degree",
    )(first, tile_count.reshape(1, blocks), tiles)
    sib_inv_root = swap(inv_root, "dev", 1)
    lists = pl.pallas_call(
        join_kernel,
        out_shape=jax.ShapeDtypeStruct((chips, cap, peers), jnp.int32),
        in_specs=[VMEM] * chips,
        out_specs=VMEM,
        compiler_params=limit(1),
        cost_estimate=pl.CostEstimate(flops=2 * 10**9, bytes_accessed=0, transcendentals=0),
        name="join",
    )(*lists)
    sends = pl.pallas_call(
        functools.partial(select_kernel, masks),
        out_shape=[jax.ShapeDtypeStruct((2, cap, k_dim, cols), BF16)] * chips,
        in_specs=[VMEM] * 5,
        out_specs=[VMEM] * chips,
        compiler_params=limit(2),
        name="select",
    )(lists, subspace, sib_columns, inv_root, sib_inv_root)
    parts = [swap(x, "dev", mask) if mask else x for x, mask in zip(sends, masks, strict=True)]

    plan = pl.pallas_call(
        plan_kernel,
        out_shape=[pltpu.SMEM(x.shape, x.dtype) for x in (tile_count, tile_slot)],
        in_specs=[HBM] * 2,
        out_specs=[SMEM] * 2,
        scratch_shapes=[pltpu.SemaphoreType.DMA((2,))],
        compiler_params=limit(1),
        cost_estimate=pl.CostEstimate(flops=2 * 10**9, bytes_accessed=0, transcendentals=0),
        name="plan",
    )(*(pltpu.with_memory_space_constraint(x, pltpu.HBM) for x in (tile_count, tile_slot)))
    plan = [pltpu.with_memory_space_constraint(x, pltpu.SMEM) for x in plan]

    applied, gram = pl.pallas_call(
        functools.partial(product_kernel, masks),
        out_shape=(
            jax.ShapeDtypeStruct((2 * k_dim, row_count), BF16),
            jax.ShapeDtypeStruct((k_dim // 2, 2 * k_dim), F32),
        ),
        in_specs=[SMEM, SMEM] + [VMEM] * (chips + 2),
        out_specs=(VMEM, VMEM),
        scratch_shapes=[pltpu.VMEM((peers * cap + 1, k_dim, cols), BF16)],
        compiler_params=limit(4),
        cost_estimate=pl.CostEstimate(
            flops=2 * tiles.size * k_dim, bytes_accessed=2 * tiles.size, transcendentals=0
        ),
        name="product",
    )(*plan, inv_root, tiles, *parts)

    gram = sum_all(gram)

    return pl.pallas_call(
        solve_kernel,
        out_shape=jax.ShapeDtypeStruct((k_dim, row_count), F32),
        in_specs=[VMEM] * 2,
        out_specs=VMEM,
        compiler_params=limit(4),
        name="solve",
    )(gram, applied)


def solution(mesh):
    placed = (
        P(None, ("grp", "dev")),
        P(("grp", "dev"), None, None, None),
        P(("grp", "dev")),
        P(("grp", "dev"), None),
        P(("grp", "dev"), None, None),
    )
    return jax.shard_map(
        body, mesh=mesh, in_specs=placed, out_specs=P(None, ("grp", "dev")), check_vma=False
    )
```

```python
import functools

import jax
import jax.numpy as jnp
from jax import lax
from jax.experimental import pallas as pl
from jax.experimental.pallas import tpu as pltpu
from jax.sharding import PartitionSpec as P

GROUP = 4
SOLVE_PARTS = 4
VMEM = pl.BlockSpec(memory_space=pltpu.VMEM)
HBM = pl.BlockSpec(memory_space=pltpu.HBM)
SMEM = pl.BlockSpec(memory_space=pltpu.SMEM)
NT = (((1,), (1,)), ((), ()))
F32 = jnp.float32
BF16 = jnp.bfloat16


def limit(mib):
    return pltpu.CompilerParams(vmem_limit_bytes=mib << 20)


def split(x):
    high = x.astype(BF16)
    return high, (x - high.astype(F32)).astype(BF16)


def start_kernel(out_ref):
    out_ref[...] = jnp.zeros_like(out_ref)


def degree_kernel(first_ref, count_ref, tiles_ref, inv_ref):
    blocks, slots, rows, cols = tiles_ref.shape
    ones = jnp.ones((8, 2 * cols), BF16)
    slot_of_lane = lax.broadcasted_iota(jnp.int32, (8, slots * cols), 1) // cols
    for b in range(blocks):
        count = count_ref[:, b : b + 1]
        tiles = [tiles_ref[b, t] for t in range(slots)]
        if b % 2:
            total = sum(
                tile.astype(F32) * (t < count).astype(F32) for t, tile in enumerate(tiles)
            )
            live, row = ones, split(total)
        else:
            live = (slot_of_lane < count).astype(F32).astype(BF16)
            row = tiles
        degree = lax.dot_general(
            live, jnp.concatenate(row, axis=1), NT, preferred_element_type=F32
        )
        inv_ref[b : b + 1] = lax.rsqrt(degree[:1])


def join_kernel(*refs):
    for i, ref in enumerate(refs[:-1]):
        refs[-1][i] = ref[0]


def select_kernel(masks, lists_ref, sub_ref, sib_sub_ref, inv_ref, sib_inv_ref, *send_refs):
    cap, cols = lists_ref.shape[1], inv_ref.shape[1]
    me = lax.axis_index("dev")
    sources = ((me, sub_ref, inv_ref), (me ^ 1, sib_sub_ref, sib_inv_ref))
    peer = lax.broadcasted_iota(jnp.int32, (1, lists_ref.shape[2]), 1)

    def block_id(chip, j, source):
        return jnp.sum(jnp.where(peer == source, lists_ref[chip, j : j + 1], 0))

    ids = [
        [block_id(mask // 2, j, source) for source, _, _ in sources for j in range(cap)]
        for mask in masks
    ]
    for blocks, send in zip(ids, send_refs, strict=True):
        scaled = []
        for i, block in enumerate(blocks):
            _, columns, inv = sources[i // cap]
            lanes = pl.ds(pl.multiple_of(block * cols, cols), cols)
            scaled.append(columns[:, lanes].astype(F32) * inv[pl.ds(block, 1), :])
        for i, block in enumerate(scaled):
            send[i // cap, i % cap] = block.astype(BF16)


def plan_kernel(count_hbm, slot_hbm, count_ref, slot_ref, sems):
    copies = [
        pltpu.make_async_copy(count_hbm, count_ref, sems.at[0]),
        pltpu.make_async_copy(slot_hbm, slot_ref, sems.at[1]),
    ]
    for copy in copies:
        copy.start()
    for copy in copies:
        copy.wait()


def product_kernel(masks, count_ref, slot_ref, inv_ref, tiles_ref, *refs):
    *part_refs, applied_ref, gram_ref, table = refs
    blocks, slots, rows, cols = tiles_ref.shape
    _, cap, k_dim, _ = part_refs[0].shape
    me = lax.axis_index("dev")
    dead = table.shape[0] - 1
    table[dead] = jnp.zeros((k_dim, cols), BF16)
    for mask, part in zip(masks, part_refs, strict=True):
        for core in range(2):
            for j in range(cap):
                table[((mask + core) ^ me) * cap + j] = part[core, j]
    for first in range(0, blocks, GROUP):
        group = range(first, first + GROUP)
        parts, tiles = [], []
        for b in group:
            count = count_ref[b]
            entries = [jnp.where(t < count, slot_ref[b, t], dead) for t in range(slots)]
            parts.append(jnp.concatenate([table[entry] for entry in entries], axis=1))
            tiles.append(jnp.concatenate([tiles_ref[b, t] for t in range(slots)], axis=1))
        total = lax.dot_general(
            jnp.concatenate(parts, axis=0),
            jnp.concatenate(tiles, axis=0),
            NT,
            preferred_element_type=F32,
        )
        for i, b in enumerate(group):
            lanes = slice(b * rows, (b + 1) * rows)
            own = total[i * k_dim : (i + 1) * k_dim, i * rows : (i + 1) * rows]
            high, low = split(own * inv_ref[b : b + 1])
            applied_ref[:k_dim, lanes] = high
            applied_ref[k_dim:, lanes] = low
    both = applied_ref[...]
    wide = lax.dot_general(both, both, NT, preferred_element_type=F32)
    wide = wide[:k_dim] + wide[k_dim:]
    gram = wide[:, :k_dim] + wide[:, k_dim:]
    half = k_dim // 2
    gram_ref[...] = jnp.concatenate([gram[:half], gram[half:]], axis=1)


def inverse_factor(gram):
    k_dim = gram.shape[0]
    wide, groups = 2 * k_dim, k_dim // 8
    square = (k_dim, k_dim)
    eye = (
        lax.broadcasted_iota(jnp.int32, square, 0) == lax.broadcasted_iota(jnp.int32, square, 1)
    ).astype(F32)
    diagonal = gram * eye
    row_scale = lax.rsqrt(jnp.sum(diagonal, axis=1, keepdims=True))
    col_scale = lax.rsqrt(jnp.sum(diagonal, axis=0, keepdims=True))
    whole = jnp.concatenate([gram * row_scale * col_scale, eye * col_scale], axis=1)
    rows = [whole[8 * i : 8 * i + 8] for i in range(groups)]
    row_ids = lax.broadcasted_iota(jnp.int32, (8, wide), 0)

    def spread(x):
        return jnp.broadcast_to(x, (8, wide))

    for g in range(groups):
        column = {
            (i, b): spread(rows[i][:, 8 * g + b : 8 * g + b + 1])
            for i in range(g, groups)
            for b in range(8)
        }
        out = rows[g]
        for s in range(0, 8, 2):
            row0, row1 = spread(rows[g][s : s + 1]), spread(rows[g][s + 1 : s + 2])
            pivot0 = {b: spread(column[g, b][s : s + 1]) for b in range(s, 8)}
            pivot1 = {b: spread(column[g, b][s + 1 : s + 2]) for b in range(s, 8)}
            p00, p01, p11 = pivot0[s], pivot0[s + 1], pivot1[s + 1]
            det = p00 * p11 - p01 * p01
            inv_det = 1.0 / det
            q00, q01, q11 = p11 * inv_det, p01 * inv_det, p00 * inv_det
            root0 = lax.rsqrt(p00)
            ratio = p01 * (root0 * root0)
            root1 = lax.rsqrt(p11 - p01 * ratio)
            out = jnp.where(row_ids == s, row0 * root0, out)
            out = jnp.where(row_ids == s + 1, (row1 - ratio * row0) * root1, out)
            for i in range(g, groups):
                x, y = column[i, s], column[i, s + 1]
                f0, f1 = q00 * x - q01 * y, q11 * y - q01 * x
                if i == g:
                    f0 = jnp.where(row_ids > s + 1, f0, 0.0)
                    f1 = jnp.where(row_ids > s + 1, f1, 0.0)
                rows[i] = rows[i] - f0 * row0 - f1 * row1
                for b in range(s + 2, 8):
                    column[i, b] = column[i, b] - f0 * pivot0[b] - f1 * pivot1[b]
        yield out[:, k_dim:]


def solve_kernel(gram_ref, applied_ref, out_hbm, out_ref, sems):
    k_dim = gram_ref.shape[1] // 2
    parts = sems.shape[0]
    packed = gram_ref[...]
    gram = jnp.concatenate([packed[:, :k_dim], packed[:, k_dim:]], axis=0)
    applied = jnp.concatenate([applied_ref[...], applied_ref[:k_dim]], axis=0)
    done, copies = [], []
    for rows in inverse_factor(gram):
        done.append(rows)
        if len(done) * 8 * parts < k_dim:
            continue
        high, low = split(jnp.concatenate(done, axis=0))
        part = pl.ds(len(copies) * 8 * len(done), 8 * len(done))
        out_ref[part] = jnp.dot(
            jnp.concatenate([high, high, low], axis=1), applied, preferred_element_type=F32
        )
        copies.append(pltpu.make_async_copy(out_ref.at[part], out_hbm.at[part], sems.at[len(copies)]))
        copies[-1].start()
        done = []
    for copy in copies:
        copy.wait()


def swap(x, axis, mask, odd_mask=None):
    odd = mask if odd_mask is None else odd_mask
    size = lax.axis_size(axis)
    core = lax.axis_size("dev") if axis != "dev" else 1
    if odd_mask is None or axis == "dev":
        return lax.ppermute(x, axis, [(i, i ^ (odd if i % 2 else mask)) for i in range(size)])
    pairs = [(i, i ^ (core * (odd if i % 2 else mask))) for i in range(size * core)]
    return lax.ppermute(x, (axis, "dev"), pairs)


def stages(axis):
    masks = [1 << i for i in range(axis == "dev", lax.axis_size(axis).bit_length() - 1)]
    return [masks[i : i + 2] for i in range(0, len(masks), 2)]


def sum_all(x):
    x = x + swap(x, "dev", 1)
    for axis in ("dev", "grp"):
        for masks in stages(axis):
            if len(masks) == 1:
                parts = [swap(x, axis, masks[0])]
            else:
                mine = swap(x, axis, masks[0], masks[0] ^ masks[1])
                both = swap(x, axis, masks[1])
                parts = [mine, both, swap(mine, "dev", 1)]
            x = x + sum(parts)
    return x


def body(subspace, tiles, tile_count, tile_slot, fetch_list):
    k_dim, row_count = subspace.shape
    blocks, slots, rows, cols = tiles.shape
    peers = lax.axis_size("dev")
    cap = fetch_list.shape[2]
    chips = peers // 2
    lists = jnp.transpose(fetch_list, (0, 2, 1))
    masks = [0] + [2 * i for i in reversed(range(1, chips))]
    lists = [lists] + [swap(lists, "dev", 2 * i) for i in range(1, chips)]
    sib_columns = swap(subspace, "dev", 1)

    first = pl.pallas_call(
        start_kernel,
        out_shape=jax.ShapeDtypeStruct((8, 128), F32),
        out_specs=VMEM,
        compiler_params=limit(1),
        cost_estimate=pl.CostEstimate(flops=10**10, bytes_accessed=0, transcendentals=0),
        name="start",
    )()
    inv_root = pl.pallas_call(
        degree_kernel,
        out_shape=jax.ShapeDtypeStruct((blocks, rows), F32),
        in_specs=[VMEM] * 3,
        out_specs=VMEM,
        compiler_params=limit(4),
        cost_estimate=pl.CostEstimate(
            flops=16 * tiles.size, bytes_accessed=2 * tiles.size, transcendentals=0
        ),
        name="degree",
    )(first, tile_count.reshape(1, blocks), tiles)
    sib_inv_root = swap(inv_root, "dev", 1)
    lists = pl.pallas_call(
        join_kernel,
        out_shape=jax.ShapeDtypeStruct((chips, cap, peers), jnp.int32),
        in_specs=[VMEM] * chips,
        out_specs=VMEM,
        compiler_params=limit(1),
        cost_estimate=pl.CostEstimate(flops=2 * 10**9, bytes_accessed=0, transcendentals=0),
        name="join",
    )(*lists)
    sends = pl.pallas_call(
        functools.partial(select_kernel, masks),
        out_shape=[jax.ShapeDtypeStruct((2, cap, k_dim, cols), BF16)] * chips,
        in_specs=[VMEM] * 5,
        out_specs=[VMEM] * chips,
        compiler_params=limit(2),
        name="select",
    )(lists, subspace, sib_columns, inv_root, sib_inv_root)
    parts = [swap(x, "dev", mask) if mask else x for x, mask in zip(sends, masks, strict=True)]

    plan = pl.pallas_call(
        plan_kernel,
        out_shape=[pltpu.SMEM(x.shape, x.dtype) for x in (tile_count, tile_slot)],
        in_specs=[HBM] * 2,
        out_specs=[SMEM] * 2,
        scratch_shapes=[pltpu.SemaphoreType.DMA((2,))],
        compiler_params=limit(1),
        cost_estimate=pl.CostEstimate(flops=2 * 10**9, bytes_accessed=0, transcendentals=0),
        name="plan",
    )(*(pltpu.with_memory_space_constraint(x, pltpu.HBM) for x in (tile_count, tile_slot)))
    plan = [pltpu.with_memory_space_constraint(x, pltpu.SMEM) for x in plan]

    applied, gram = pl.pallas_call(
        functools.partial(product_kernel, masks),
        out_shape=(
            jax.ShapeDtypeStruct((2 * k_dim, row_count), BF16),
            jax.ShapeDtypeStruct((k_dim // 2, 2 * k_dim), F32),
        ),
        in_specs=[SMEM, SMEM] + [VMEM] * (chips + 2),
        out_specs=(VMEM, VMEM),
        scratch_shapes=[pltpu.VMEM((peers * cap + 1, k_dim, cols), BF16)],
        compiler_params=limit(4),
        cost_estimate=pl.CostEstimate(
            flops=2 * tiles.size * k_dim, bytes_accessed=2 * tiles.size, transcendentals=0
        ),
        name="product",
    )(*plan, inv_root, tiles, *parts)

    gram = sum_all(gram)

    return pl.pallas_call(
        solve_kernel,
        out_shape=jax.ShapeDtypeStruct((k_dim, row_count), F32),
        in_specs=[VMEM] * 2,
        out_specs=HBM,
        scratch_shapes=[
            pltpu.VMEM((k_dim, row_count), F32),
            pltpu.SemaphoreType.DMA((SOLVE_PARTS,)),
        ],
        compiler_params=limit(4),
        name="solve",
    )(gram, applied)


def solution(mesh):
    placed = (
        P(None, ("grp", "dev")),
        P(("grp", "dev"), None, None, None),
        P(("grp", "dev")),
        P(("grp", "dev"), None),
        P(("grp", "dev"), None, None),
    )
    return jax.shard_map(
        body, mesh=mesh, in_specs=placed, out_specs=P(None, ("grp", "dev")), check_vma=False
    )
```

```python
import functools

import jax
import jax.numpy as jnp
from jax import lax
from jax.experimental import pallas as pl
from jax.experimental.pallas import tpu as pltpu
from jax.sharding import PartitionSpec as P

GROUP = 4
SOLVE_PARTS = 4
VMEM = pl.BlockSpec(memory_space=pltpu.VMEM)
HBM = pl.BlockSpec(memory_space=pltpu.HBM)
SMEM = pl.BlockSpec(memory_space=pltpu.SMEM)
NT = (((1,), (1,)), ((), ()))
F32 = jnp.float32
BF16 = jnp.bfloat16


def limit(mib):
    return pltpu.CompilerParams(vmem_limit_bytes=mib << 20)


def split(x):
    high = x.astype(BF16)
    return high, (x - high.astype(F32)).astype(BF16)


def start_kernel(out_ref):
    out_ref[...] = jnp.zeros_like(out_ref)


def degree_kernel(first_ref, count_ref, tiles_ref, inv_ref):
    blocks, slots, rows, cols = tiles_ref.shape
    ones = jnp.ones((8, 2 * cols), BF16)
    slot_of_lane = lax.broadcasted_iota(jnp.int32, (8, slots * cols), 1) // cols
    for b in range(blocks):
        count = count_ref[:, b : b + 1]
        tiles = [tiles_ref[b, t] for t in range(slots)]
        if b % 2:
            total = sum(
                tile.astype(F32) * (t < count).astype(F32) for t, tile in enumerate(tiles)
            )
            live, row = ones, split(total)
        else:
            live = (slot_of_lane < count).astype(F32).astype(BF16)
            row = tiles
        degree = lax.dot_general(
            live, jnp.concatenate(row, axis=1), NT, preferred_element_type=F32
        )
        inv_ref[b : b + 1] = lax.rsqrt(degree[:1])


def join_kernel(*refs):
    for i, ref in enumerate(refs[:-1]):
        refs[-1][i] = ref[0]


def select_kernel(masks, lists_ref, sub_ref, sib_sub_ref, inv_ref, sib_inv_ref, *send_refs):
    cap, cols = lists_ref.shape[1], inv_ref.shape[1]
    me = lax.axis_index("dev")
    sources = ((me, sub_ref, inv_ref), (me ^ 1, sib_sub_ref, sib_inv_ref))
    peer = lax.broadcasted_iota(jnp.int32, (1, lists_ref.shape[2]), 1)

    def block_id(chip, j, source):
        return jnp.sum(jnp.where(peer == source, lists_ref[chip, j : j + 1], 0))

    ids = [
        [block_id(mask // 2, j, source) for source, _, _ in sources for j in range(cap)]
        for mask in masks
    ]
    for blocks, send in zip(ids, send_refs, strict=True):
        scaled = []
        for i, block in enumerate(blocks):
            _, columns, inv = sources[i // cap]
            lanes = pl.ds(pl.multiple_of(block * cols, cols), cols)
            scaled.append(columns[:, lanes].astype(F32) * inv[pl.ds(block, 1), :])
        for i, block in enumerate(scaled):
            send[i // cap, i % cap] = block.astype(BF16)


def plan_kernel(count_hbm, slot_hbm, count_ref, slot_ref, sems):
    copies = [
        pltpu.make_async_copy(count_hbm, count_ref, sems.at[0]),
        pltpu.make_async_copy(slot_hbm, slot_ref, sems.at[1]),
    ]
    for copy in copies:
        copy.start()
    for copy in copies:
        copy.wait()


def product_kernel(masks, count_ref, slot_ref, inv_ref, tiles_ref, *refs):
    *part_refs, applied_ref, gram_ref, table = refs
    blocks, slots, rows, cols = tiles_ref.shape
    _, cap, k_dim, _ = part_refs[0].shape
    me = lax.axis_index("dev")
    dead = table.shape[0] - 1
    table[dead] = jnp.zeros((k_dim, cols), BF16)
    for mask, part in zip(masks, part_refs, strict=True):
        for core in range(2):
            for j in range(cap):
                table[((mask + core) ^ me) * cap + j] = part[core, j]
    for first in range(0, blocks, GROUP):
        group = range(first, first + GROUP)
        parts, tiles = [], []
        for b in group:
            count = count_ref[b]
            entries = [jnp.where(t < count, slot_ref[b, t], dead) for t in range(slots)]
            parts.append(jnp.concatenate([table[entry] for entry in entries], axis=1))
            tiles.append(jnp.concatenate([tiles_ref[b, t] for t in range(slots)], axis=1))
        total = lax.dot_general(
            jnp.concatenate(parts, axis=0),
            jnp.concatenate(tiles, axis=0),
            NT,
            preferred_element_type=F32,
        )
        for i, b in enumerate(group):
            lanes = slice(b * rows, (b + 1) * rows)
            own = total[i * k_dim : (i + 1) * k_dim, i * rows : (i + 1) * rows]
            high, low = split(own * inv_ref[b : b + 1])
            applied_ref[:k_dim, lanes] = high
            applied_ref[k_dim:, lanes] = low
    both = applied_ref[...]
    wide = lax.dot_general(both, both, NT, preferred_element_type=F32)
    wide = wide[:k_dim] + wide[k_dim:]
    gram = wide[:, :k_dim] + wide[:, k_dim:]
    half = k_dim // 2
    gram_ref[...] = jnp.concatenate([gram[:half], gram[half:]], axis=1)


def inverse_factor(gram):
    k_dim = gram.shape[0]
    wide, groups = 2 * k_dim, k_dim // 8
    square = (k_dim, k_dim)
    eye = (
        lax.broadcasted_iota(jnp.int32, square, 0) == lax.broadcasted_iota(jnp.int32, square, 1)
    ).astype(F32)
    diagonal = gram * eye
    row_scale = lax.rsqrt(jnp.sum(diagonal, axis=1, keepdims=True))
    col_scale = lax.rsqrt(jnp.sum(diagonal, axis=0, keepdims=True))
    whole = jnp.concatenate([gram * row_scale * col_scale, eye * col_scale], axis=1)
    rows = [whole[8 * i : 8 * i + 8] for i in range(groups)]
    row_ids = lax.broadcasted_iota(jnp.int32, (8, wide), 0)

    def spread(x):
        return jnp.broadcast_to(x, (8, wide))

    for g in range(groups):
        column = {
            (i, b): spread(rows[i][:, 8 * g + b : 8 * g + b + 1])
            for i in range(g, groups)
            for b in range(8)
        }
        out = rows[g]
        for s in range(0, 8, 2):
            row0, row1 = spread(rows[g][s : s + 1]), spread(rows[g][s + 1 : s + 2])
            pivot0 = {b: spread(column[g, b][s : s + 1]) for b in range(s, 8)}
            pivot1 = {b: spread(column[g, b][s + 1 : s + 2]) for b in range(s, 8)}
            p00, p01, p11 = pivot0[s], pivot0[s + 1], pivot1[s + 1]
            det = p00 * p11 - p01 * p01
            inv_det = 1.0 / det
            q00, q01, q11 = p11 * inv_det, p01 * inv_det, p00 * inv_det
            root0 = lax.rsqrt(p00)
            ratio = p01 * (root0 * root0)
            root1 = lax.rsqrt(p11 - p01 * ratio)
            out = jnp.where(row_ids == s, row0 * root0, out)
            out = jnp.where(row_ids == s + 1, (row1 - ratio * row0) * root1, out)
            for i in range(g, groups):
                x, y = column[i, s], column[i, s + 1]
                f0, f1 = q00 * x - q01 * y, q11 * y - q01 * x
                if i == g:
                    f0 = jnp.where(row_ids > s + 1, f0, 0.0)
                    f1 = jnp.where(row_ids > s + 1, f1, 0.0)
                rows[i] = rows[i] - f0 * row0 - f1 * row1
                for b in range(s + 2, 8):
                    column[i, b] = column[i, b] - f0 * pivot0[b] - f1 * pivot1[b]
        yield out[:, k_dim:]


def solve_kernel(gram_ref, applied_ref, out_hbm, out_ref, sems):
    k_dim = gram_ref.shape[1] // 2
    parts = sems.shape[0]
    packed = gram_ref[...]
    gram = jnp.concatenate([packed[:, :k_dim], packed[:, k_dim:]], axis=0)
    applied = jnp.concatenate([applied_ref[...], applied_ref[:k_dim]], axis=0)
    done, copies = [], []
    for rows in inverse_factor(gram):
        done.append(rows)
        if len(done) * 8 * parts < k_dim:
            continue
        high, low = split(jnp.concatenate(done, axis=0))
        part = pl.ds(len(copies) * 8 * len(done), 8 * len(done))
        out_ref[part] = jnp.dot(
            jnp.concatenate([high, high, low], axis=1), applied, preferred_element_type=F32
        )
        copies.append(pltpu.make_async_copy(out_ref.at[part], out_hbm.at[part], sems.at[len(copies)]))
        copies[-1].start()
        done = []
    for copy in copies:
        copy.wait()


def swap(x, axis, mask, odd_mask=None):
    odd = mask if odd_mask is None else odd_mask
    size = lax.axis_size(axis)
    core = lax.axis_size("dev") if axis != "dev" else 1
    if odd_mask is None or axis == "dev":
        return lax.ppermute(x, axis, [(i, i ^ (odd if i % 2 else mask)) for i in range(size)])
    pairs = [(i, i ^ (core * (odd if i % 2 else mask))) for i in range(size * core)]
    return lax.ppermute(x, (axis, "dev"), pairs)


def stages(axis):
    masks = [1 << i for i in range(axis == "dev", lax.axis_size(axis).bit_length() - 1)]
    return [masks[i : i + 2] for i in range(0, len(masks), 2)]


def sum_all(x):
    x = x + swap(x, "dev", 1)
    for axis in ("grp", "dev"):
        for masks in stages(axis):
            if len(masks) == 1:
                parts = [swap(x, axis, masks[0])]
            else:
                mine = swap(x, axis, masks[0], masks[0] ^ masks[1])
                both = swap(x, axis, masks[1])
                parts = [mine, both, swap(mine, "dev", 1)]
            x = x + sum(parts)
    return x


def body(subspace, tiles, tile_count, tile_slot, fetch_list):
    k_dim, row_count = subspace.shape
    blocks, slots, rows, cols = tiles.shape
    peers = lax.axis_size("dev")
    cap = fetch_list.shape[2]
    chips = peers // 2
    lists = jnp.transpose(fetch_list, (0, 2, 1))
    masks = [0] + [2 * i for i in reversed(range(1, chips))]
    lists = [lists] + [swap(lists, "dev", 2 * i) for i in range(1, chips)]
    sib_columns = swap(subspace, "dev", 1)

    first = pl.pallas_call(
        start_kernel,
        out_shape=jax.ShapeDtypeStruct((8, 128), F32),
        out_specs=VMEM,
        compiler_params=limit(1),
        cost_estimate=pl.CostEstimate(flops=10**10, bytes_accessed=0, transcendentals=0),
        name="start",
    )()
    inv_root = pl.pallas_call(
        degree_kernel,
        out_shape=jax.ShapeDtypeStruct((blocks, rows), F32),
        in_specs=[VMEM] * 3,
        out_specs=VMEM,
        compiler_params=limit(4),
        cost_estimate=pl.CostEstimate(
            flops=16 * tiles.size, bytes_accessed=2 * tiles.size, transcendentals=0
        ),
        name="degree",
    )(first, tile_count.reshape(1, blocks), tiles)
    sib_inv_root = swap(inv_root, "dev", 1)
    lists = pl.pallas_call(
        join_kernel,
        out_shape=jax.ShapeDtypeStruct((chips, cap, peers), jnp.int32),
        in_specs=[VMEM] * chips,
        out_specs=VMEM,
        compiler_params=limit(1),
        cost_estimate=pl.CostEstimate(flops=2 * 10**9, bytes_accessed=0, transcendentals=0),
        name="join",
    )(*lists)
    sends = pl.pallas_call(
        functools.partial(select_kernel, masks),
        out_shape=[jax.ShapeDtypeStruct((2, cap, k_dim, cols), BF16)] * chips,
        in_specs=[VMEM] * 5,
        out_specs=[VMEM] * chips,
        compiler_params=limit(2),
        name="select",
    )(lists, subspace, sib_columns, inv_root, sib_inv_root)
    parts = [swap(x, "dev", mask) if mask else x for x, mask in zip(sends, masks, strict=True)]

    plan = pl.pallas_call(
        plan_kernel,
        out_shape=[pltpu.SMEM(x.shape, x.dtype) for x in (tile_count, tile_slot)],
        in_specs=[HBM] * 2,
        out_specs=[SMEM] * 2,
        scratch_shapes=[pltpu.SemaphoreType.DMA((2,))],
        compiler_params=limit(1),
        cost_estimate=pl.CostEstimate(flops=2 * 10**9, bytes_accessed=0, transcendentals=0),
        name="plan",
    )(*(pltpu.with_memory_space_constraint(x, pltpu.HBM) for x in (tile_count, tile_slot)))
    plan = [pltpu.with_memory_space_constraint(x, pltpu.SMEM) for x in plan]

    applied, gram = pl.pallas_call(
        functools.partial(product_kernel, masks),
        out_shape=(
            jax.ShapeDtypeStruct((2 * k_dim, row_count), BF16),
            jax.ShapeDtypeStruct((k_dim // 2, 2 * k_dim), F32),
        ),
        in_specs=[SMEM, SMEM] + [VMEM] * (chips + 2),
        out_specs=(VMEM, VMEM),
        scratch_shapes=[pltpu.VMEM((peers * cap + 1, k_dim, cols), BF16)],
        compiler_params=limit(4),
        cost_estimate=pl.CostEstimate(
            flops=2 * tiles.size * k_dim, bytes_accessed=2 * tiles.size, transcendentals=0
        ),
        name="product",
    )(*plan, inv_root, tiles, *parts)

    gram = sum_all(gram)

    return pl.pallas_call(
        solve_kernel,
        out_shape=jax.ShapeDtypeStruct((k_dim, row_count), F32),
        in_specs=[VMEM] * 2,
        out_specs=HBM,
        scratch_shapes=[
            pltpu.VMEM((k_dim, row_count), F32),
            pltpu.SemaphoreType.DMA((SOLVE_PARTS,)),
        ],
        compiler_params=limit(4),
        name="solve",
    )(gram, applied)


def solution(mesh):
    placed = (
        P(None, ("grp", "dev")),
        P(("grp", "dev"), None, None, None),
        P(("grp", "dev")),
        P(("grp", "dev"), None),
        P(("grp", "dev"), None, None),
    )
    return jax.shard_map(
        body, mesh=mesh, in_specs=placed, out_specs=P(None, ("grp", "dev")), check_vma=False
    )
```
